32 devices in a mesh: dp: 4 (over y, x), cent: 4 (over z), rep: 2 (over core).
Axes of the slice: x: 2, y: 2, z: 4, core: 2. Of those that a mesh axis runs over, the one named last changes fastest.
Arguments:
- rows: bfloat16 [16384, 1024], P(('dp', 'rep')), may hold values from -15 to 15
- panel: bfloat16 [4096, 1024], P('cent'), may hold values from -2.15 to 2.15
- scales: float32 [4096, 8], P('cent'), may hold values from 0.7 to 1.4
- inv_temp: int32 [1], replicated, may hold values from 4 to 15
Outputs:
- centroid_sums: float32 [1024, 4096], P(('dp', 'rep'), 'cent')
- centroid_counts: float32 [4096], P('cent')
The draws below stay inside these ranges and needn't reach their ends.
All inputs are finite; a program needn't handle non-finite values.
Results may differ from the reference program's by a relative error of at most 0.04.
Values may be sent and summed in bfloat16 or wider, within the bound.
A program may use at most 64 MiB of HBM per device.

```python
import math
import jax
import jax.numpy as jnp
from jax import lax

D = 1024
BLOCK = 128
CENTROIDS = 4096
ROWS = 16384


def centroid_parts(key):
    signed = jax.random.uniform(jax.random.fold_in(key, 11), (CENTROIDS, D), jnp.float32, -1.0, 1.0)
    target = jnp.where(signed < 0.0, signed - 0.5, signed + 0.5)
    logs = jax.random.uniform(jax.random.fold_in(key, 12), (CENTROIDS, D // BLOCK), jnp.float32, math.log(0.7), math.log(1.4))
    scales = jnp.exp(logs)
    panel = (target.reshape(CENTROIDS, D // BLOCK, BLOCK) / scales[:, :, None]).reshape(CENTROIDS, D)
    return (panel, scales)


def draw_panel(key, part):
    panel, scales = centroid_parts(key)
    return panel.astype(jnp.bfloat16)


def draw_scales(key, part):
    panel, scales = centroid_parts(key)
    return scales


def draw_rows(key, part):
    panel, scales = centroid_parts(key)
    rounded = panel.astype(jnp.bfloat16).astype(jnp.float32)
    full = (rounded.reshape(CENTROIDS, D // BLOCK, BLOCK) * scales[:, :, None]).reshape(CENTROIDS, D)
    first = jax.random.randint(jax.random.fold_in(key, 23), (ROWS,), 0, CENTROIDS)
    strength = jax.random.uniform(jax.random.fold_in(key, 25), (ROWS, 1), jnp.float32, 1.0, 4.9)
    spread = jax.random.uniform(jax.random.fold_in(key, 24), (ROWS, 1), jnp.float32, 0.0, 3.0)
    extra = jnp.clip(jax.random.normal(jax.random.fold_in(key, 26), (ROWS, D), jnp.float32), -2.5, 2.5)
    mixed = strength * full[first] + spread * extra
    chosen = (jnp.arange(ROWS) % 64 == 0)[:, None]
    drawn = jnp.clip(jax.random.normal(jax.random.fold_in(key, 21), (ROWS, D), jnp.float32), -4.0, 4.0)
    values = jnp.where(chosen, mixed, drawn)
    return values.astype(jnp.bfloat16)


def setup_inputs(seed: int = 0) -> dict:
    streams_of = jax.random.split(jax.random.key(seed), 5)
    return {
        "rows": draw_rows(jax.random.fold_in(streams_of[4], 71), 0),
        "panel": draw_panel(jax.random.fold_in(streams_of[4], 71), 0),
        "scales": draw_scales(jax.random.fold_in(streams_of[4], 71), 0),
        "inv_temp": jax.random.randint(streams_of[3], (1,), 4, 16).astype(jnp.int32),
    }


def dequantize(panel, scales):
    count, width = panel.shape
    blocks = scales.shape[1]
    full = panel.astype(jnp.float32).reshape(count, blocks, width // blocks) * scales[:, :, None]
    return full.reshape(count, width).astype(jnp.bfloat16)

def reference(rows, panel, scales, inv_temp):
    centroids = dequantize(panel, scales)
    norms = lax.optimization_barrier(jnp.sum(centroids.astype(jnp.float32) ** 2, axis=1))
    factor = inv_temp[0].astype(jnp.float32) / math.sqrt(D)
    blk = math.gcd(ROWS, 512)
    stacked = rows.reshape(ROWS // blk, blk, D)

    def step(carry, row_block):
        prod = lax.dot_general(row_block, centroids, (((1,), (1,)), ((), ())), preferred_element_type=jnp.float32)
        logits = (prod - 0.5 * norms[None, :]) * factor
        row_max = lax.optimization_barrier(jnp.max(logits, axis=1))
        expo = jnp.exp(logits - row_max[:, None])
        row_total = lax.optimization_barrier(jnp.sum(expo, axis=1))
        weights = (expo / row_total[:, None]).astype(jnp.bfloat16)
        sums = carry[0] + lax.dot_general(row_block, weights, (((0,), (0,)), ((), ())), preferred_element_type=jnp.float32)
        counts = carry[1] + lax.optimization_barrier(jnp.sum(weights.astype(jnp.float32), axis=0))
        return ((sums, counts), None)
    init = (jnp.zeros((D, CENTROIDS), jnp.float32), jnp.zeros((CENTROIDS,), jnp.float32))
    (sums, counts), _ = lax.scan(step, init, stacked)
    return (sums, counts)
```

```python
import functools
import math

import jax
import jax.numpy as jnp
from jax import lax
from jax.experimental import pallas as pl
from jax.experimental.pallas import tpu as pltpu
from jax.sharding import PartitionSpec as P

MESH = pl.DeviceIdType.MESH
NT = (((1,), (1,)), ((), ()))
NN = (((1,), (0,)), ((), ()))
LANES = 128


def flip(index, mask, bits):
    for b in range(bits):
        if (mask >> b) & 1:
            index = index + (1 << b) - (2 << b) * ((index // (1 << b)) % 2)
    return index


def first_step(q, order):
    for j, b in enumerate(order):
        if (q >> b) & 1:
            return j
    return len(order)


def kernel(dp_n, cent_n, rep_n, parts,
           rows_hbm, panel_hbm, scales_ref, temp_ref,
           out_ref, counts_ref, *scratch):
    n_chunks, tile = parts
    scratch = list(scratch)
    rows_ref, panel_ref, cent_ref, bias_ref, w_ref, cnt_ref = scratch[:6]
    t_refs = scratch[6:6 + n_chunks]
    (own_ref, core_out, core_in, dp_out, dp_in, stat_out, stat_in, cnt_out, cnt_in,
     rows_sem, panel_sem, core_ss, core_rs, dp_ss, dp_rs, stat_ss, stat_rs,
     cnt_ss, cnt_rs) = scratch[6 + n_chunks:]

    n_rows, width = rows_ref.shape
    n_cent = cent_ref.shape[0]
    n = n_rows // n_chunks
    n_blk = scales_ref.shape[1]
    blk = width // n_blk
    fb = out_ref.shape[1]
    half = n_cent // 2
    bits = dp_n.bit_length() - 1

    d = lax.axis_index("dp")
    z = lax.axis_index("cent")
    r = lax.axis_index("rep")

    panel_copy = pltpu.make_async_copy(panel_hbm, panel_ref, panel_sem)
    panel_copy.start()
    row_copies = []
    for c in range(n_chunks):
        cp = pltpu.make_async_copy(
            rows_hbm.at[pl.ds(c * n, n)], rows_ref.at[pl.ds(c * n, n)], rows_sem.at[c])
        cp.start()
        row_copies.append(cp)

    z_peers = [lax.rem(z + o, cent_n) for o in range(1, cent_n)]
    group = [(lax.rem(d + o // rep_n, dp_n), lax.rem(r + o % rep_n, rep_n))
             for o in range(1, dp_n * rep_n)]
    barrier = pltpu.get_barrier_semaphore()
    for peer in z_peers:
        pl.semaphore_signal(barrier, inc=1, device_id={"cent": peer}, device_id_type=MESH)
    for pd, pr in group:
        pl.semaphore_signal(barrier, inc=1, device_id={"dp": pd, "rep": pr}, device_id_type=MESH)

    scale2 = temp_ref[0].astype(jnp.float32) * (math.log2(math.e) / math.sqrt(width))

    panel_copy.wait()
    for k in range(0, n_cent, tile):
        sq = jnp.zeros((tile, blk), jnp.float32)
        for b in range(n_blk):
            full = panel_ref[k:k + tile, b * blk:(b + 1) * blk].astype(jnp.float32)
            full = (full * scales_ref[k:k + tile, b:b + 1]).astype(jnp.bfloat16)
            cent_ref[k:k + tile, b * blk:(b + 1) * blk] = full
            wide = full.astype(jnp.float32)
            sq = sq + wide * wide
        norm = jnp.sum(sq, axis=1, keepdims=True)
        bias_ref[k:k + tile, :] = jnp.broadcast_to((-0.5 * scale2) * norm, (tile, LANES))

    pl.semaphore_wait(barrier, len(z_peers) + len(group))

    stat_copies = []

    def logits_tile(c, k):
        prod = lax.dot_general(cent_ref[k:k + tile, :], rows_ref[c * n:(c + 1) * n, :], NT,
                               preferred_element_type=jnp.float32)
        bias = jnp.concatenate([bias_ref[k:k + tile, :]] * (n // LANES), axis=1)
        t = prod * scale2 + bias
        t_refs[c][k:k + tile, :] = t
        return jnp.max(t.reshape(tile // 8, 8, n), axis=0)

    def exp_tile(c, k, top):
        e = jnp.exp2(t_refs[c][k:k + tile, :] - top)
        t_refs[c][k:k + tile, :] = e
        return jnp.sum(e.reshape(tile // 8, 8, n), axis=0)

    def send_stats(c, top, total):
        stat_out[c, 0:1, :] = top
        stat_out[c, 1:2, :] = total
        for o, peer in enumerate(z_peers):
            cp = pltpu.make_async_remote_copy(
                stat_out.at[c], stat_in.at[c, o], stat_ss.at[c, o], stat_rs.at[c, o],
                device_id={"cent": peer}, device_id_type=MESH)
            cp.start()
            stat_copies.append(cp)

    tops = [None] * n_chunks
    for c in range(n_chunks + 1):
        if c < n_chunks:
            row_copies[c].wait()
        best = total = None
        for k in range(0, n_cent, tile):
            if c < n_chunks:
                m = logits_tile(c, k)
                best = m if best is None else jnp.maximum(best, m)
            if c > 0:
                s = exp_tile(c - 1, k, tops[c - 1])
                total = s if total is None else total + s
        if c < n_chunks:
            tops[c] = jnp.max(best, axis=0, keepdims=True)
        if c > 0:
            send_stats(c - 1, tops[c - 1], jnp.sum(total, axis=0, keepdims=True))

    def weights(c):
        for cp in stat_copies[c * len(z_peers):(c + 1) * len(z_peers)]:
            cp.wait_recv()
        mine = stat_out[c, 0:1, :]
        top = mine
        for o in range(len(z_peers)):
            top = jnp.maximum(top, stat_in[c, o, 0:1, :])
        total = stat_out[c, 1:2, :] * jnp.exp2(mine - top)
        for o in range(len(z_peers)):
            total = total + stat_in[c, o, 1:2, :] * jnp.exp2(stat_in[c, o, 0:1, :] - top)
        ratio = jnp.exp2(mine - top) / total
        for k in range(0, n_cent, tile):
            w = t_refs[c][k:k + tile, :] * ratio
            w_ref[k:k + tile, c * n:(c + 1) * n] = w.astype(jnp.bfloat16)
            part = w[:, :LANES]
            for l in range(LANES, n, LANES):
                part = part + w[:, l:l + LANES]
            if c > 0:
                part = part + cnt_ref[k:k + tile, :]
            cnt_ref[k:k + tile, :] = part

    def columns(q):
        return pl.ds(pl.multiple_of(flip(d, q, bits) * (2 * fb), 2 * fb), 2 * fb)

    core_copies = {}
    dp_copies = {}

    def split(h, q, prod):
        first = r == 0
        own_ref[h, q] = jnp.where(first, prod[:, :fb], prod[:, fb:])
        core_out[h, q] = jnp.where(first, prod[:, fb:], prod[:, :fb]).astype(jnp.bfloat16)
        cp = pltpu.make_async_remote_copy(
            core_out.at[h, q], core_in.at[h, q], core_ss.at[h, q], core_rs.at[h, q],
            device_id={"rep": 1 - r}, device_id_type=MESH)
        cp.start()
        core_copies[h, q] = cp

    orders = [list(range(bits)), list(range(bits))[::-1]]

    def unit(h, q):
        split(h, q, lax.dot_general(w_ref[h * half:(h + 1) * half, :], rows_ref[:, columns(q)], NN,
                                    preferred_element_type=jnp.float32))

    def finish(h, q):
        order = orders[h]
        j = first_step(q, order)
        core_copies[h, q].wait_recv()
        total = own_ref[h, q] + core_in[h, q].astype(jnp.float32)
        for i in range(j):
            src = q ^ (1 << order[i])
            dp_copies[h, src].wait_recv()
            total = total + dp_in[h, src - 1].astype(jnp.float32)
        if q == 0:
            out_ref[h * half:(h + 1) * half, :] = total
            return
        dp_out[h, q - 1] = total.astype(jnp.bfloat16)
        cp = pltpu.make_async_remote_copy(
            dp_out.at[h, q - 1], dp_in.at[h, q - 1], dp_ss.at[h, q - 1], dp_rs.at[h, q - 1],
            device_id={"dp": flip(d, 1 << order[j], bits)}, device_id_type=MESH)
        cp.start()
        dp_copies[h, q] = cp

    ranked = []
    for order in orders:
        ranked.append(sorted(range(dp_n), reverse=True,
                             key=lambda q: [(q >> b) & 1 for b in order]))
    todo = [(h, ranked[h][i]) for i in range(dp_n) for h in range(2)]

    acc = None
    h0, q0 = todo[0]
    for c in range(n_chunks):
        weights(c)
        p = lax.dot_general(w_ref[h0 * half:(h0 + 1) * half, c * n:(c + 1) * n],
                            rows_ref[c * n:(c + 1) * n, columns(q0)], NN,
                            preferred_element_type=jnp.float32)
        acc = p if acc is None else acc + p
    split(h0, q0, acc)

    cnt_out[...] = jnp.sum(cnt_ref[...].T, axis=0, keepdims=True)
    cnt_copies = []
    for o, (pd, pr) in enumerate(group):
        cp = pltpu.make_async_remote_copy(
            cnt_out, cnt_in.at[o], cnt_ss.at[o], cnt_rs.at[o],
            device_id={"dp": pd, "rep": pr}, device_id_type=MESH)
        cp.start()
        cnt_copies.append(cp)

    done = 0
    for i in range(1, len(todo)):
        unit(*todo[i])
        h, q = todo[done]
        if done < i and first_step(q, orders[h]) == 0:
            finish(h, q)
            done += 1
    for h, q in todo[done:-2]:
        finish(h, q)

    counts = cnt_out[...]
    for o, cp in enumerate(cnt_copies):
        cp.wait_recv()
        counts = counts + cnt_in[o]
    counts_ref[...] = counts

    for h, q in todo[-2:]:
        finish(h, q)

    for cp in stat_copies + cnt_copies + list(core_copies.values()) + list(dp_copies.values()):
        cp.wait_send()


def on_device(sizes, rows, panel, scales, inv_temp):
    dp_n, cent_n, rep_n = sizes
    n_rows, width = rows.shape
    n_cent = panel.shape[0]
    n_chunks = 4
    tile = 256
    n = n_rows // n_chunks
    fb = width // (dp_n * rep_n)
    half = n_cent // 2
    group = dp_n * rep_n - 1
    f32, bf16 = jnp.float32, jnp.bfloat16
    dma = pltpu.SemaphoreType.DMA
    body = functools.partial(kernel, dp_n, cent_n, rep_n, (n_chunks, tile))
    sums, counts = pl.pallas_call(
        body,
        out_shape=(jax.ShapeDtypeStruct((n_cent, fb), f32), jax.ShapeDtypeStruct((1, n_cent), f32)),
        in_specs=[pl.BlockSpec(memory_space=pl.ANY), pl.BlockSpec(memory_space=pl.ANY),
                  pl.BlockSpec(memory_space=pltpu.VMEM), pl.BlockSpec(memory_space=pltpu.SMEM)],
        out_specs=(pl.BlockSpec(memory_space=pltpu.VMEM), pl.BlockSpec(memory_space=pltpu.VMEM)),
        scratch_shapes=[
            pltpu.VMEM((n_rows, width), bf16),
            pltpu.VMEM((n_cent, width), bf16),
            pltpu.VMEM((n_cent, width), bf16),
            pltpu.VMEM((n_cent, LANES), f32),
            pltpu.VMEM((n_cent, n_rows), bf16),
            pltpu.VMEM((n_cent, LANES), f32),
            *[pltpu.VMEM((n_cent, n), f32) for _ in range(n_chunks)],
            pltpu.VMEM((2, dp_n, half, fb), f32),
            pltpu.VMEM((2, dp_n, half, fb), bf16),
            pltpu.VMEM((2, dp_n, half, fb), bf16),
            pltpu.VMEM((2, dp_n - 1, half, fb), bf16),
            pltpu.VMEM((2, dp_n - 1, half, fb), bf16),
            pltpu.VMEM((n_chunks, 2, n), f32),
            pltpu.VMEM((n_chunks, cent_n - 1, 2, n), f32),
            pltpu.VMEM((1, n_cent), f32),
            pltpu.VMEM((group, 1, n_cent), f32),
            dma((n_chunks,)), dma,
            dma((2, dp_n)), dma((2, dp_n)),
            dma((2, dp_n - 1)), dma((2, dp_n - 1)),
            dma((n_chunks, cent_n - 1)), dma((n_chunks, cent_n - 1)),
            dma((group,)), dma((group,)),
        ],
        compiler_params=pltpu.CompilerParams(
            collective_id=0, has_side_effects=True, vmem_limit_bytes=56 * 1024 * 1024),
    )(rows, panel, scales, inv_temp)
    return sums.T, counts.reshape(n_cent)


def solution(mesh):
    sizes = (mesh.shape["dp"], mesh.shape["cent"], mesh.shape["rep"])
    in_specs = (P(("dp", "rep"), None), P("cent", None), P("cent", None), P())
    out_specs = (P(("dp", "rep"), "cent"), P("cent"))
    return jax.shard_map(
        functools.partial(on_device, sizes), mesh=mesh, in_specs=in_specs, out_specs=out_specs,
        check_vma=False,
    )
```

```python
import functools
import math

import jax
import jax.numpy as jnp
from jax import lax
from jax.experimental import pallas as pl
from jax.experimental.pallas import tpu as pltpu
from jax.sharding import PartitionSpec as P

MESH = pl.DeviceIdType.MESH
NT = (((1,), (1,)), ((), ()))
NN = (((1,), (0,)), ((), ()))
LANES = 128


def flip(index, mask, bits):
    for b in range(bits):
        if (mask >> b) & 1:
            index = index + (1 << b) - (2 << b) * ((index // (1 << b)) % 2)
    return index


def first_step(q, order):
    for j, b in enumerate(order):
        if (q >> b) & 1:
            return j
    return len(order)


def kernel(dp_n, cent_n, rep_n, parts,
           rows_hbm, panel_hbm, scales_ref, temp_ref,
           out_ref, counts_ref, *scratch):
    n_chunks, tile = parts
    scratch = list(scratch)
    rows_ref, panel_ref, cent_ref, bias_ref, w_ref, cnt_ref = scratch[:6]
    t_refs = scratch[6:6 + n_chunks]
    (own_ref, core_out, core_in, dp_out, dp_in, stat_out, stat_in, cnt_out, cnt_in,
     rows_sem, panel_sem, core_ss, core_rs, dp_ss, dp_rs, stat_ss, stat_rs,
     cnt_ss, cnt_rs) = scratch[6 + n_chunks:]

    n_rows, width = rows_ref.shape
    n_cent = cent_ref.shape[0]
    n = n_rows // n_chunks
    n_blk = scales_ref.shape[0]
    blk = width // n_blk
    fb = out_ref.shape[1]
    half = n_cent // 2
    bits = dp_n.bit_length() - 1

    d = lax.axis_index("dp")
    z = lax.axis_index("cent")
    r = lax.axis_index("rep")

    panel_copies = []
    for i, k in enumerate(range(0, n_cent, tile)):
        cp = pltpu.make_async_copy(
            panel_hbm.at[pl.ds(k, tile)], panel_ref.at[pl.ds(k, tile)], panel_sem.at[i])
        cp.start()
        panel_copies.append(cp)
    row_copies = []
    for c in range(n_chunks):
        cp = pltpu.make_async_copy(
            rows_hbm.at[pl.ds(c * n, n)], rows_ref.at[pl.ds(c * n, n)], rows_sem.at[c])
        cp.start()
        row_copies.append(cp)

    z_peers = [lax.rem(z + o, cent_n) for o in range(1, cent_n)]
    group = [(lax.rem(d + o // rep_n, dp_n), lax.rem(r + o % rep_n, rep_n))
             for o in range(1, dp_n * rep_n)]
    barrier = pltpu.get_barrier_semaphore()
    for peer in z_peers:
        pl.semaphore_signal(barrier, inc=1, device_id={"cent": peer}, device_id_type=MESH)
    for pd, pr in group:
        pl.semaphore_signal(barrier, inc=1, device_id={"dp": pd, "rep": pr}, device_id_type=MESH)

    scale2 = temp_ref[0].astype(jnp.float32) * (math.log2(math.e) / math.sqrt(width))

    scales = scales_ref[...].T
    for i, k in enumerate(range(0, n_cent, tile)):
        panel_copies[i].wait()
        sq = jnp.zeros((tile, blk), jnp.float32)
        for b in range(n_blk):
            full = panel_ref[k:k + tile, b * blk:(b + 1) * blk].astype(jnp.float32)
            full = (full * scales[k:k + tile, b:b + 1]).astype(jnp.bfloat16)
            cent_ref[k:k + tile, b * blk:(b + 1) * blk] = full
            wide = full.astype(jnp.float32)
            sq = sq + wide * wide
        norm = jnp.sum(sq, axis=1, keepdims=True)
        bias_ref[k:k + tile, :] = jnp.broadcast_to((-0.5 * scale2) * norm, (tile, LANES))

    pl.semaphore_wait(barrier, len(z_peers) + len(group))

    stat_copies = []

    def logits(c):
        prod = lax.dot_general(cent_ref[...], rows_ref[c * n:(c + 1) * n, :], NT,
                               preferred_element_type=jnp.float32)
        best = None
        for k in range(0, n_cent, tile):
            bias = jnp.concatenate([bias_ref[k:k + tile, :]] * (n // LANES), axis=1)
            t = prod[k:k + tile, :] * scale2 + bias
            t_refs[c][k:k + tile, :] = t
            m = jnp.max(t.reshape(tile // 8, 8, n), axis=0)
            best = m if best is None else jnp.maximum(best, m)
        return jnp.max(best, axis=0, keepdims=True)

    def exp_tile(c, k, top):
        e = jnp.exp2(t_refs[c][k:k + tile, :] - top)
        t_refs[c][k:k + tile, :] = e
        return jnp.sum(e.reshape(tile // 8, 8, n), axis=0)

    def send_stats(c, top, total):
        stat_out[c, 0:1, :] = top
        stat_out[c, 1:2, :] = total
        for o, peer in enumerate(z_peers):
            cp = pltpu.make_async_remote_copy(
                stat_out.at[c], stat_in.at[c, o], stat_ss.at[c, o], stat_rs.at[c, o],
                device_id={"cent": peer}, device_id_type=MESH)
            cp.start()
            stat_copies.append(cp)

    def ratios(c):
        for cp in stat_copies[c * len(z_peers):(c + 1) * len(z_peers)]:
            cp.wait_recv()
        mine = stat_out[c, 0:1, :]
        top = mine
        for o in range(len(z_peers)):
            top = jnp.maximum(top, stat_in[c, o, 0:1, :])
        total = stat_out[c, 1:2, :] * jnp.exp2(mine - top)
        for o in range(len(z_peers)):
            total = total + stat_in[c, o, 1:2, :] * jnp.exp2(stat_in[c, o, 0:1, :] - top)
        return jnp.exp2(mine - top) / total

    def weights(c, ratio):
        for k in range(0, n_cent, tile):
            w = t_refs[c][k:k + tile, :] * ratio
            w_ref[k:k + tile, c * n:(c + 1) * n] = w.astype(jnp.bfloat16)
            part = w[:, :LANES]
            for l in range(LANES, n, LANES):
                part = part + w[:, l:l + LANES]
            if c > 0:
                part = part + cnt_ref[k:k + tile, :]
            cnt_ref[k:k + tile, :] = part

    lag = 3
    tops = []
    for c in range(n_chunks + 1):
        if c < n_chunks:
            row_copies[c].wait()
        if c >= lag:
            ratio = ratios(c - lag)
        if c < n_chunks:
            tops.append(logits(c))
        if c > 0:
            total = None
            for k in range(0, n_cent, tile):
                part = exp_tile(c - 1, k, tops[c - 1])
                total = part if total is None else total + part
        if c >= lag:
            weights(c - lag, ratio)
        if c > 0:
            send_stats(c - 1, tops[c - 1], jnp.sum(total, axis=0, keepdims=True))

    def columns(q):
        return pl.ds(pl.multiple_of(flip(d, q, bits) * (2 * fb), 2 * fb), 2 * fb)

    core_copies = {}
    dp_copies = {}

    def split(h, q, prod):
        first = r == 0
        own_ref[h, q] = jnp.where(first, prod[:, :fb], prod[:, fb:])
        core_out[h, q] = jnp.where(first, prod[:, fb:], prod[:, :fb]).astype(jnp.bfloat16)
        cp = pltpu.make_async_remote_copy(
            core_out.at[h, q], core_in.at[h, q], core_ss.at[h, q], core_rs.at[h, q],
            device_id={"rep": 1 - r}, device_id_type=MESH)
        cp.start()
        core_copies[h, q] = cp

    orders = [list(range(bits)), list(range(bits))[::-1]]

    def dot(start, stop, q):
        return lax.dot_general(w_ref[:, start:stop], rows_ref[start:stop, columns(q)], NN,
                               preferred_element_type=jnp.float32)

    def unit(q, prod):
        for h in range(2):
            split(h, q, prod[h * half:(h + 1) * half])

    def finish(h, q):
        order = orders[h]
        j = first_step(q, order)
        core_copies[h, q].wait_recv()
        total = own_ref[h, q] + core_in[h, q].astype(jnp.float32)
        for i in range(j):
            src = q ^ (1 << order[i])
            dp_copies[h, src].wait_recv()
            total = total + dp_in[h, src - 1].astype(jnp.float32)
        if q == 0:
            out_ref[h * half:(h + 1) * half, :] = total
            return
        dp_out[h, q - 1] = total.astype(jnp.bfloat16)
        cp = pltpu.make_async_remote_copy(
            dp_out.at[h, q - 1], dp_in.at[h, q - 1], dp_ss.at[h, q - 1], dp_rs.at[h, q - 1],
            device_id={"dp": flip(d, 1 << order[j], bits)}, device_id_type=MESH)
        cp.start()
        dp_copies[h, q] = cp

    ranked = [sorted(range(dp_n), reverse=True, key=lambda q: [(q >> b) & 1 for b in order])
              for order in orders]

    early = n_chunks + 1 - lag
    prod = dot(0, early * n, ranked[0][0])
    for c in range(early, n_chunks):
        weights(c, ratios(c))
    unit(ranked[0][0], prod + dot(early * n, n_rows, ranked[0][0]))

    cnt_out[...] = jnp.sum(cnt_ref[...].T, axis=0, keepdims=True)
    cnt_copies = []
    for o, (pd, pr) in enumerate(group):
        cp = pltpu.make_async_remote_copy(
            cnt_out, cnt_in.at[o], cnt_ss.at[o], cnt_rs.at[o],
            device_id={"dp": pd, "rep": pr}, device_id_type=MESH)
        cp.start()
        cnt_copies.append(cp)

    for i in range(1, dp_n):
        unit(ranked[0][i], dot(0, n_rows, ranked[0][i]))
        for h in range(2):
            if first_step(ranked[0][i - 1], orders[h]) == 0:
                finish(h, ranked[0][i - 1])
    later = [(first_step(q, orders[h]), i, h, q) for h in range(2)
             for i, q in enumerate(ranked[h]) if first_step(q, orders[h]) > 0]
    later.sort()
    for _, _, h, q in later[:-2]:
        finish(h, q)

    counts = cnt_out[...]
    for o, cp in enumerate(cnt_copies):
        cp.wait_recv()
        counts = counts + cnt_in[o]
    counts_ref[...] = counts

    for _, _, h, q in later[-2:]:
        finish(h, q)

    for cp in stat_copies + cnt_copies + list(core_copies.values()) + list(dp_copies.values()):
        cp.wait_send()


def place(sums_ref, counts_in, out_ref, counts_ref):
    out_ref[...] = sums_ref[...].T
    counts_ref[...] = counts_in[...]


def on_device(sizes, rows, panel, scales, inv_temp):
    dp_n, cent_n, rep_n = sizes
    n_rows, width = rows.shape
    n_cent = panel.shape[0]
    n_chunks = 8
    tile = 256
    n = n_rows // n_chunks
    fb = width // (dp_n * rep_n)
    half = n_cent // 2
    group = dp_n * rep_n - 1
    f32, bf16 = jnp.float32, jnp.bfloat16
    dma = pltpu.SemaphoreType.DMA
    body = functools.partial(kernel, dp_n, cent_n, rep_n, (n_chunks, tile))
    sums, counts = pl.pallas_call(
        body,
        out_shape=(jax.ShapeDtypeStruct((n_cent, fb), f32), jax.ShapeDtypeStruct((1, n_cent), f32)),
        in_specs=[pl.BlockSpec(memory_space=pl.ANY), pl.BlockSpec(memory_space=pl.ANY),
                  pl.BlockSpec(memory_space=pltpu.VMEM), pl.BlockSpec(memory_space=pltpu.SMEM)],
        out_specs=(pl.BlockSpec(memory_space=pltpu.VMEM), pl.BlockSpec(memory_space=pltpu.VMEM)),
        scratch_shapes=[
            pltpu.VMEM((n_rows, width), bf16),
            pltpu.VMEM((n_cent, width), bf16),
            pltpu.VMEM((n_cent, width), bf16),
            pltpu.VMEM((n_cent, LANES), f32),
            pltpu.VMEM((n_cent, n_rows), bf16),
            pltpu.VMEM((n_cent, LANES), f32),
            *[pltpu.VMEM((n_cent, n), f32) for _ in range(n_chunks)],
            pltpu.VMEM((2, dp_n, half, fb), f32),
            pltpu.VMEM((2, dp_n, half, fb), bf16),
            pltpu.VMEM((2, dp_n, half, fb), bf16),
            pltpu.VMEM((2, dp_n - 1, half, fb), bf16),
            pltpu.VMEM((2, dp_n - 1, half, fb), bf16),
            pltpu.VMEM((n_chunks, 2, n), f32),
            pltpu.VMEM((n_chunks, cent_n - 1, 2, n), f32),
            pltpu.VMEM((1, n_cent), f32),
            pltpu.VMEM((group, 1, n_cent), f32),
            dma((n_chunks,)), dma((n_cent // tile,)),
            dma((2, dp_n)), dma((2, dp_n)),
            dma((2, dp_n - 1)), dma((2, dp_n - 1)),
            dma((n_chunks, cent_n - 1)), dma((n_chunks, cent_n - 1)),
            dma((group,)), dma((group,)),
        ],
        compiler_params=pltpu.CompilerParams(
            collective_id=0, has_side_effects=True, vmem_limit_bytes=56 * 1024 * 1024),
    )(rows, panel, scales.T, inv_temp)
    sums, counts = pl.pallas_call(
        place,
        out_shape=(jax.ShapeDtypeStruct((fb, n_cent), f32), jax.ShapeDtypeStruct((1, n_cent), f32)),
        in_specs=[pl.BlockSpec(memory_space=pltpu.VMEM)] * 2,
        out_specs=(pl.BlockSpec(memory_space=pltpu.VMEM),) * 2,
    )(sums, counts)
    return sums, counts.reshape(n_cent)


def solution(mesh):
    sizes = (mesh.shape["dp"], mesh.shape["cent"], mesh.shape["rep"])
    in_specs = (P(("dp", "rep"), None), P("cent", None), P("cent", None), P())
    out_specs = (P(("dp", "rep"), "cent"), P("cent"))
    return jax.shard_map(
        functools.partial(on_device, sizes), mesh=mesh, in_specs=in_specs, out_specs=out_specs,
        check_vma=False,
    )
```

```python
import functools
import math

import jax
import jax.numpy as jnp
from jax import lax
from jax.experimental import pallas as pl
from jax.experimental.pallas import tpu as pltpu
from jax.sharding import PartitionSpec as P

MESH = pl.DeviceIdType.MESH
NT = (((1,), (1,)), ((), ()))
NN = (((1,), (0,)), ((), ()))
LANES = 128


def flip(index, mask, bits):
    for b in range(bits):
        if (mask >> b) & 1:
            index = index + (1 << b) - (2 << b) * ((index // (1 << b)) % 2)
    return index


def first_step(q, order):
    for j, b in enumerate(order):
        if (q >> b) & 1:
            return j
    return len(order)


def kernel(dp_n, cent_n, rep_n, parts,
           rows_hbm, panel_hbm, scales_ref, temp_ref,
           out_ref, counts_ref, *scratch):
    n_chunks, tile = parts
    scratch = list(scratch)
    rows_ref, panel_ref, cent_ref, bias_ref, w_ref, cnt_ref = scratch[:6]
    t_refs = scratch[6:6 + n_chunks]
    (own_ref, core_out, core_in, dp_out, dp_in, stat_out, stat_in, cnt_out, cnt_in,
     rows_sem, panel_sem, core_ss, core_rs, dp_ss, dp_rs, stat_ss, stat_rs,
     cnt_ss, cnt_rs) = scratch[6 + n_chunks:]

    n_rows, width = rows_ref.shape
    n_cent = cent_ref.shape[0]
    n = n_rows // n_chunks
    n_blk = scales_ref.shape[0]
    blk = width // n_blk
    fb = out_ref.shape[1]
    half = n_cent // 2
    bits = dp_n.bit_length() - 1

    d = lax.axis_index("dp")
    z = lax.axis_index("cent")
    r = lax.axis_index("rep")

    panel_copies = []
    for i, k in enumerate(range(0, n_cent, tile)):
        cp = pltpu.make_async_copy(
            panel_hbm.at[pl.ds(k, tile)], panel_ref.at[pl.ds(k, tile)], panel_sem.at[i])
        cp.start()
        panel_copies.append(cp)
    row_copies = []
    for c in range(n_chunks):
        cp = pltpu.make_async_copy(
            rows_hbm.at[pl.ds(c * n, n)], rows_ref.at[pl.ds(c * n, n)], rows_sem.at[c])
        cp.start()
        row_copies.append(cp)

    z_peers = [lax.rem(z + o, cent_n) for o in range(1, cent_n)]
    group = [(lax.rem(d + o // rep_n, dp_n), lax.rem(r + o % rep_n, rep_n))
             for o in range(1, dp_n * rep_n)]
    barrier = pltpu.get_barrier_semaphore()
    for peer in z_peers:
        pl.semaphore_signal(barrier, inc=1, device_id={"cent": peer}, device_id_type=MESH)
    for pd, pr in group:
        pl.semaphore_signal(barrier, inc=1, device_id={"dp": pd, "rep": pr}, device_id_type=MESH)

    scale2 = temp_ref[0].astype(jnp.float32) * (math.log2(math.e) / math.sqrt(width))

    scales = scales_ref[...].T
    for i, k in enumerate(range(0, n_cent, tile)):
        panel_copies[i].wait()
        sq = jnp.zeros((tile, blk), jnp.float32)
        for b in range(n_blk):
            full = panel_ref[k:k + tile, b * blk:(b + 1) * blk].astype(jnp.float32)
            full = (full * scales[k:k + tile, b:b + 1]).astype(jnp.bfloat16)
            cent_ref[k:k + tile, b * blk:(b + 1) * blk] = full
            wide = full.astype(jnp.float32)
            sq = sq + wide * wide
        norm = jnp.sum(sq, axis=1, keepdims=True)
        bias_ref[k:k + tile, :] = jnp.broadcast_to((-0.5 * scale2) * norm, (tile, LANES))

    pl.semaphore_wait(barrier, len(z_peers) + len(group))

    stat_copies = []

    def logits_tile(c, k):
        prod = lax.dot_general(cent_ref[k:k + tile, :], rows_ref[c * n:(c + 1) * n, :], NT,
                               preferred_element_type=jnp.float32)
        bias = jnp.concatenate([bias_ref[k:k + tile, :]] * (n // LANES), axis=1)
        t = prod * scale2 + bias
        t_refs[c][k:k + tile, :] = t
        return jnp.max(t.reshape(tile // 8, 8, n), axis=0)

    def exp_tile(c, k, top):
        e = jnp.exp2(t_refs[c][k:k + tile, :] - top)
        t_refs[c][k:k + tile, :] = e
        return jnp.sum(e.reshape(tile // 8, 8, n), axis=0)

    def send_stats(c, top, total):
        stat_out[c, 0:1, :] = top
        stat_out[c, 1:2, :] = total
        for o, peer in enumerate(z_peers):
            cp = pltpu.make_async_remote_copy(
                stat_out.at[c], stat_in.at[c, o], stat_ss.at[c, o], stat_rs.at[c, o],
                device_id={"cent": peer}, device_id_type=MESH)
            cp.start()
            stat_copies.append(cp)

    def ratios(c):
        for cp in stat_copies[c * len(z_peers):(c + 1) * len(z_peers)]:
            cp.wait_recv()
        mine = stat_out[c, 0:1, :]
        top = mine
        for o in range(len(z_peers)):
            top = jnp.maximum(top, stat_in[c, o, 0:1, :])
        total = stat_out[c, 1:2, :] * jnp.exp2(mine - top)
        for o in range(len(z_peers)):
            total = total + stat_in[c, o, 1:2, :] * jnp.exp2(stat_in[c, o, 0:1, :] - top)
        return jnp.exp2(mine - top) / total

    def weights_tile(c, k, ratio):
        w = t_refs[c][k:k + tile, :] * ratio
        w_ref[k:k + tile, c * n:(c + 1) * n] = w.astype(jnp.bfloat16)
        part = w[:, :LANES]
        for l in range(LANES, n, LANES):
            part = part + w[:, l:l + LANES]
        if c > 0:
            part = part + cnt_ref[k:k + tile, :]
        cnt_ref[k:k + tile, :] = part

    def weights(c, ratio):
        for k in range(0, n_cent, tile):
            weights_tile(c, k, ratio)

    lag = 3
    tops = []
    for c in range(n_chunks + 1):
        if c < n_chunks:
            row_copies[c].wait()
        if c >= lag:
            ratio = ratios(c - lag)
        best = total = None
        for k in range(0, n_cent, tile):
            if c < n_chunks:
                m = logits_tile(c, k)
                best = m if best is None else jnp.maximum(best, m)
            if c > 0:
                part = exp_tile(c - 1, k, tops[c - 1])
                total = part if total is None else total + part
            if c >= lag:
                weights_tile(c - lag, k, ratio)
        if c < n_chunks:
            tops.append(jnp.max(best, axis=0, keepdims=True))
        if c > 0:
            send_stats(c - 1, tops[c - 1], jnp.sum(total, axis=0, keepdims=True))

    def columns(q):
        return pl.ds(pl.multiple_of(flip(d, q, bits) * (2 * fb), 2 * fb), 2 * fb)

    core_copies = {}
    dp_copies = {}

    first = r == 0
    orders = [list(range(bits)), list(range(bits))[::-1]]

    def dot(start, stop, k, q):
        return lax.dot_general(w_ref[k:k + tile, start:stop], rows_ref[start:stop, columns(q)], NN,
                               preferred_element_type=jnp.float32)

    def unit(q):
        for h in range(2):
            for k in range(0, half, tile):
                prod = dot(0, n_rows, h * half + k, q)
                own_ref[h, q, k:k + tile, :] = jnp.where(first, prod[:, :fb], prod[:, fb:])
                core_out[h, q, k:k + tile, :] = jnp.where(
                    first, prod[:, fb:], prod[:, :fb]).astype(jnp.bfloat16)
            cp = pltpu.make_async_remote_copy(
                core_out.at[h, q], core_in.at[h, q], core_ss.at[h, q], core_rs.at[h, q],
                device_id={"rep": 1 - r}, device_id_type=MESH)
            cp.start()
            core_copies[h, q] = cp

    def finish(h, q):
        order = orders[h]
        j = first_step(q, order)
        core_copies[h, q].wait_recv()
        total = own_ref[h, q] + core_in[h, q].astype(jnp.float32)
        for i in range(j):
            src = q ^ (1 << order[i])
            dp_copies[h, src].wait_recv()
            total = total + dp_in[h, src - 1].astype(jnp.float32)
        if q == 0:
            out_ref[h * half:(h + 1) * half, :] = total
            return
        dp_out[h, q - 1] = total.astype(jnp.bfloat16)
        cp = pltpu.make_async_remote_copy(
            dp_out.at[h, q - 1], dp_in.at[h, q - 1], dp_ss.at[h, q - 1], dp_rs.at[h, q - 1],
            device_id={"dp": flip(d, 1 << order[j], bits)}, device_id_type=MESH)
        cp.start()
        dp_copies[h, q] = cp

    ranked = [sorted(range(dp_n), reverse=True, key=lambda q: [(q >> b) & 1 for b in order])
              for order in orders]

    for c in range(n_chunks + 1 - lag, n_chunks):
        weights(c, ratios(c))
    unit(ranked[0][0])

    cnt_out[...] = jnp.sum(cnt_ref[...].T, axis=0, keepdims=True)
    cnt_copies = []
    for o, (pd, pr) in enumerate(group):
        cp = pltpu.make_async_remote_copy(
            cnt_out, cnt_in.at[o], cnt_ss.at[o], cnt_rs.at[o],
            device_id={"dp": pd, "rep": pr}, device_id_type=MESH)
        cp.start()
        cnt_copies.append(cp)

    for i in range(1, dp_n):
        unit(ranked[0][i])
        for h in range(2):
            if first_step(ranked[0][i - 1], orders[h]) == 0:
                finish(h, ranked[0][i - 1])
    later = [(first_step(q, orders[h]), i, h, q) for h in range(2)
             for i, q in enumerate(ranked[h]) if first_step(q, orders[h]) > 0]
    later.sort()
    for _, _, h, q in later[:-2]:
        finish(h, q)

    counts = cnt_out[...]
    for o, cp in enumerate(cnt_copies):
        cp.wait_recv()
        counts = counts + cnt_in[o]
    counts_ref[...] = counts

    for _, _, h, q in later[-2:]:
        finish(h, q)

    for cp in stat_copies + cnt_copies + list(core_copies.values()) + list(dp_copies.values()):
        cp.wait_send()


def place(sums_ref, counts_in, out_ref, counts_ref):
    out_ref[...] = sums_ref[...].T
    counts_ref[...] = counts_in[...]


def on_device(sizes, rows, panel, scales, inv_temp):
    dp_n, cent_n, rep_n = sizes
    n_rows, width = rows.shape
    n_cent = panel.shape[0]
    n_chunks = 8
    tile = 256
    n = n_rows // n_chunks
    fb = width // (dp_n * rep_n)
    half = n_cent // 2
    group = dp_n * rep_n - 1
    f32, bf16 = jnp.float32, jnp.bfloat16
    dma = pltpu.SemaphoreType.DMA
    body = functools.partial(kernel, dp_n, cent_n, rep_n, (n_chunks, tile))
    sums, counts = pl.pallas_call(
        body,
        out_shape=(jax.ShapeDtypeStruct((n_cent, fb), f32), jax.ShapeDtypeStruct((1, n_cent), f32)),
        in_specs=[pl.BlockSpec(memory_space=pl.ANY), pl.BlockSpec(memory_space=pl.ANY),
                  pl.BlockSpec(memory_space=pltpu.VMEM), pl.BlockSpec(memory_space=pltpu.SMEM)],
        out_specs=(pl.BlockSpec(memory_space=pltpu.VMEM), pl.BlockSpec(memory_space=pltpu.VMEM)),
        scratch_shapes=[
            pltpu.VMEM((n_rows, width), bf16),
            pltpu.VMEM((n_cent, width), bf16),
            pltpu.VMEM((n_cent, width), bf16),
            pltpu.VMEM((n_cent, LANES), f32),
            pltpu.VMEM((n_cent, n_rows), bf16),
            pltpu.VMEM((n_cent, LANES), f32),
            *[pltpu.VMEM((n_cent, n), f32) for _ in range(n_chunks)],
            pltpu.VMEM((2, dp_n, half, fb), f32),
            pltpu.VMEM((2, dp_n, half, fb), bf16),
            pltpu.VMEM((2, dp_n, half, fb), bf16),
            pltpu.VMEM((2, dp_n - 1, half, fb), bf16),
            pltpu.VMEM((2, dp_n - 1, half, fb), bf16),
            pltpu.VMEM((n_chunks, 2, n), f32),
            pltpu.VMEM((n_chunks, cent_n - 1, 2, n), f32),
            pltpu.VMEM((1, n_cent), f32),
            pltpu.VMEM((group, 1, n_cent), f32),
            dma((n_chunks,)), dma((n_cent // tile,)),
            dma((2, dp_n)), dma((2, dp_n)),
            dma((2, dp_n - 1)), dma((2, dp_n - 1)),
            dma((n_chunks, cent_n - 1)), dma((n_chunks, cent_n - 1)),
            dma((group,)), dma((group,)),
        ],
        compiler_params=pltpu.CompilerParams(
            collective_id=0, has_side_effects=True, vmem_limit_bytes=56 * 1024 * 1024),
    )(rows, panel, scales.T, inv_temp)
    sums, counts = pl.pallas_call(
        place,
        out_shape=(jax.ShapeDtypeStruct((fb, n_cent), f32), jax.ShapeDtypeStruct((1, n_cent), f32)),
        in_specs=[pl.BlockSpec(memory_space=pltpu.VMEM)] * 2,
        out_specs=(pl.BlockSpec(memory_space=pltpu.VMEM),) * 2,
    )(sums, counts)
    return sums, counts.reshape(n_cent)


def solution(mesh):
    sizes = (mesh.shape["dp"], mesh.shape["cent"], mesh.shape["rep"])
    in_specs = (P(("dp", "rep"), None), P("cent", None), P("cent", None), P())
    out_specs = (P(("dp", "rep"), "cent"), P("cent"))
    return jax.shard_map(
        functools.partial(on_device, sizes), mesh=mesh, in_specs=in_specs, out_specs=out_specs,
        check_vma=False,
    )
```

```python
import functools
import math

import jax
import jax.numpy as jnp
from jax import lax
from jax.experimental import pallas as pl
from jax.experimental.pallas import tpu as pltpu
from jax.sharding import PartitionSpec as P

MESH = pl.DeviceIdType.MESH
NT = (((1,), (1,)), ((), ()))
NN = (((1,), (0,)), ((), ()))
LANES = 128


def flip(index, mask, bits):
    for b in range(bits):
        if (mask >> b) & 1:
            index = index + (1 << b) - (2 << b) * ((index // (1 << b)) % 2)
    return index


def first_step(q, order):
    for j, b in enumerate(order):
        if (q >> b) & 1:
            return j
    return len(order)


def kernel(dp_n, cent_n, rep_n, parts,
           rows_hbm, panel_hbm, scales_ref, temp_ref,
           out_ref, counts_ref, *scratch):
    n_chunks, tile = parts
    scratch = list(scratch)
    rows_ref, panel_ref, cent_ref, bias_ref, w_ref, cnt_ref = scratch[:6]
    t_refs = scratch[6:6 + n_chunks]
    (early_ref, own_ref, core_out, core_in, dp_out, dp_in, stat_out, stat_in, cnt_out, cnt_in,
     rows_sem, panel_sem, core_ss, core_rs, dp_ss, dp_rs, stat_ss, stat_rs,
     cnt_ss, cnt_rs) = scratch[6 + n_chunks:]

    n_rows, width = rows_ref.shape
    n_cent = cent_ref.shape[0]
    n = n_rows // n_chunks
    n_blk = scales_ref.shape[0]
    blk = width // n_blk
    fb = out_ref.shape[1]
    half = n_cent // 2
    bits = dp_n.bit_length() - 1

    d = lax.axis_index("dp")
    z = lax.axis_index("cent")
    r = lax.axis_index("rep")

    panel_copies = []
    for i, k in enumerate(range(0, n_cent, tile)):
        cp = pltpu.make_async_copy(
            panel_hbm.at[pl.ds(k, tile)], panel_ref.at[pl.ds(k, tile)], panel_sem.at[i])
        cp.start()
        panel_copies.append(cp)
    row_copies = []
    for c in range(n_chunks):
        cp = pltpu.make_async_copy(
            rows_hbm.at[pl.ds(c * n, n)], rows_ref.at[pl.ds(c * n, n)], rows_sem.at[c])
        cp.start()
        row_copies.append(cp)

    z_peers = [lax.rem(z + o, cent_n) for o in range(1, cent_n)]
    group = [(lax.rem(d + o // rep_n, dp_n), lax.rem(r + o % rep_n, rep_n))
             for o in range(1, dp_n * rep_n)]
    barrier = pltpu.get_barrier_semaphore()
    for peer in z_peers:
        pl.semaphore_signal(barrier, inc=1, device_id={"cent": peer}, device_id_type=MESH)
    for pd, pr in group:
        pl.semaphore_signal(barrier, inc=1, device_id={"dp": pd, "rep": pr}, device_id_type=MESH)

    scale2 = temp_ref[0].astype(jnp.float32) * (math.log2(math.e) / math.sqrt(width))

    scales = scales_ref[...].T
    for i, k in enumerate(range(0, n_cent, tile)):
        panel_copies[i].wait()
        sq = jnp.zeros((tile, blk), jnp.float32)
        for b in range(n_blk):
            full = panel_ref[k:k + tile, b * blk:(b + 1) * blk].astype(jnp.float32)
            full = (full * scales[k:k + tile, b:b + 1]).astype(jnp.bfloat16)
            cent_ref[k:k + tile, b * blk:(b + 1) * blk] = full
            wide = full.astype(jnp.float32)
            sq = sq + wide * wide
        norm = jnp.sum(sq, axis=1, keepdims=True)
        bias_ref[k:k + tile, :] = jnp.broadcast_to((-0.5 * scale2) * norm, (tile, LANES))

    pl.semaphore_wait(barrier, len(z_peers) + len(group))

    stat_copies = []

    def logits_tile(c, k):
        prod = lax.dot_general(cent_ref[k:k + tile, :], rows_ref[c * n:(c + 1) * n, :], NT,
                               preferred_element_type=jnp.float32)
        bias = jnp.concatenate([bias_ref[k:k + tile, :]] * (n // LANES), axis=1)
        t = prod * scale2 + bias
        t_refs[c][k:k + tile, :] = t
        return jnp.max(t.reshape(tile // 8, 8, n), axis=0)

    def exp_tile(c, k, top):
        e = jnp.exp2(t_refs[c][k:k + tile, :] - top)
        t_refs[c][k:k + tile, :] = e
        return jnp.sum(e.reshape(tile // 8, 8, n), axis=0)

    def send_stats(c, top, total):
        stat_out[c, 0:1, :] = top
        stat_out[c, 1:2, :] = total
        for o, peer in enumerate(z_peers):
            cp = pltpu.make_async_remote_copy(
                stat_out.at[c], stat_in.at[c, o], stat_ss.at[c, o], stat_rs.at[c, o],
                device_id={"cent": peer}, device_id_type=MESH)
            cp.start()
            stat_copies.append(cp)

    def ratios(c):
        for cp in stat_copies[c * len(z_peers):(c + 1) * len(z_peers)]:
            cp.wait_recv()
        mine = stat_out[c, 0:1, :]
        top = mine
        for o in range(len(z_peers)):
            top = jnp.maximum(top, stat_in[c, o, 0:1, :])
        total = stat_out[c, 1:2, :] * jnp.exp2(mine - top)
        for o in range(len(z_peers)):
            total = total + stat_in[c, o, 1:2, :] * jnp.exp2(stat_in[c, o, 0:1, :] - top)
        return jnp.exp2(mine - top) / total

    def weights_tile(c, k, ratio):
        w = t_refs[c][k:k + tile, :] * ratio
        w_ref[k:k + tile, c * n:(c + 1) * n] = w.astype(jnp.bfloat16)
        part = w[:, :LANES]
        for l in range(LANES, n, LANES):
            part = part + w[:, l:l + LANES]
        if c > 0:
            part = part + cnt_ref[k:k + tile, :]
        cnt_ref[k:k + tile, :] = part

    def weights(c, ratio):
        for k in range(0, n_cent, tile):
            weights_tile(c, k, ratio)

    tops = []
    for c in range(n_chunks + 1):
        if c < n_chunks:
            row_copies[c].wait()
        best = total = None
        for k in range(0, n_cent, tile):
            if c < n_chunks:
                m = logits_tile(c, k)
                best = m if best is None else jnp.maximum(best, m)
            if c > 0:
                part = exp_tile(c - 1, k, tops[c - 1])
                total = part if total is None else total + part
        if c < n_chunks:
            tops.append(jnp.max(best, axis=0, keepdims=True))
        if c > 0:
            send_stats(c - 1, tops[c - 1], jnp.sum(total, axis=0, keepdims=True))

    def columns(q):
        return pl.ds(pl.multiple_of(flip(d, q, bits) * (2 * fb), 2 * fb), 2 * fb)

    core_copies = {}
    dp_copies = {}

    first = r == 0
    orders = [list(range(bits)), list(range(bits))[::-1]]

    def dot(start, stop, h, q):
        return lax.dot_general(w_ref[h * half:(h + 1) * half, start:stop],
                               rows_ref[start:stop, columns(q)], NN,
                               preferred_element_type=jnp.float32)

    def split(h, q, prod):
        own_ref[h, q] = jnp.where(first, prod[:, :fb], prod[:, fb:])
        core_out[h, q] = jnp.where(first, prod[:, fb:], prod[:, :fb]).astype(jnp.bfloat16)
        cp = pltpu.make_async_remote_copy(
            core_out.at[h, q], core_in.at[h, q], core_ss.at[h, q], core_rs.at[h, q],
            device_id={"rep": 1 - r}, device_id_type=MESH)
        cp.start()
        core_copies[h, q] = cp

    def unit(q):
        for h in range(2):
            split(h, q, dot(0, n_rows, h, q))

    def finish(h, q):
        order = orders[h]
        j = first_step(q, order)
        core_copies[h, q].wait_recv()
        total = own_ref[h, q] + core_in[h, q].astype(jnp.float32)
        for i in range(j):
            src = q ^ (1 << order[i])
            dp_copies[h, src].wait_recv()
            total = total + dp_in[h, src - 1].astype(jnp.float32)
        if q == 0:
            out_ref[h * half:(h + 1) * half, :] = total
            return
        dp_out[h, q - 1] = total.astype(jnp.bfloat16)
        cp = pltpu.make_async_remote_copy(
            dp_out.at[h, q - 1], dp_in.at[h, q - 1], dp_ss.at[h, q - 1], dp_rs.at[h, q - 1],
            device_id={"dp": flip(d, 1 << order[j], bits)}, device_id_type=MESH)
        cp.start()
        dp_copies[h, q] = cp

    ranked = [sorted(range(dp_n), reverse=True, key=lambda q: [(q >> b) & 1 for b in order])
              for order in orders]

    q0 = ranked[0][0]
    cut = (n_chunks - 1) * n
    for c in range(n_chunks - 1):
        weights(c, ratios(c))
    early = [dot(0, cut, h, q0) for h in range(2)]
    for h in range(2):
        own_ref[h, q0] = early[h][:, :fb]
        early_ref[h] = early[h][:, fb:]
    weights(n_chunks - 1, ratios(n_chunks - 1))
    for h in range(2):
        prod = jnp.concatenate([own_ref[h, q0], early_ref[h]], axis=1)
        split(h, q0, prod + dot(cut, n_rows, h, q0))

    cnt_out[...] = jnp.sum(cnt_ref[...].T, axis=0, keepdims=True)
    cnt_copies = []
    for o, (pd, pr) in enumerate(group):
        cp = pltpu.make_async_remote_copy(
            cnt_out, cnt_in.at[o], cnt_ss.at[o], cnt_rs.at[o],
            device_id={"dp": pd, "rep": pr}, device_id_type=MESH)
        cp.start()
        cnt_copies.append(cp)

    for i in range(1, dp_n):
        unit(ranked[0][i])
        for h in range(2):
            if first_step(ranked[0][i - 1], orders[h]) == 0:
                finish(h, ranked[0][i - 1])
    later = [(first_step(q, orders[h]), i, h, q) for h in range(2)
             for i, q in enumerate(ranked[h]) if first_step(q, orders[h]) > 0]
    later.sort()
    for _, _, h, q in later[:-2]:
        finish(h, q)

    counts = cnt_out[...]
    for o, cp in enumerate(cnt_copies):
        cp.wait_recv()
        counts = counts + cnt_in[o]
    counts_ref[...] = counts

    for _, _, h, q in later[-2:]:
        finish(h, q)

    for cp in stat_copies + cnt_copies + list(core_copies.values()) + list(dp_copies.values()):
        cp.wait_send()


def place(sums_ref, counts_in, out_ref, counts_ref):
    out_ref[...] = sums_ref[...].T
    counts_ref[...] = counts_in[...]


def on_device(sizes, rows, panel, scales, inv_temp):
    dp_n, cent_n, rep_n = sizes
    n_rows, width = rows.shape
    n_cent = panel.shape[0]
    n_chunks = 4
    tile = 256
    n = n_rows // n_chunks
    fb = width // (dp_n * rep_n)
    half = n_cent // 2
    group = dp_n * rep_n - 1
    f32, bf16 = jnp.float32, jnp.bfloat16
    dma = pltpu.SemaphoreType.DMA
    body = functools.partial(kernel, dp_n, cent_n, rep_n, (n_chunks, tile))
    sums, counts = pl.pallas_call(
        body,
        out_shape=(jax.ShapeDtypeStruct((n_cent, fb), f32), jax.ShapeDtypeStruct((1, n_cent), f32)),
        in_specs=[pl.BlockSpec(memory_space=pl.ANY), pl.BlockSpec(memory_space=pl.ANY),
                  pl.BlockSpec(memory_space=pltpu.VMEM), pl.BlockSpec(memory_space=pltpu.SMEM)],
        out_specs=(pl.BlockSpec(memory_space=pltpu.VMEM), pl.BlockSpec(memory_space=pltpu.VMEM)),
        scratch_shapes=[
            pltpu.VMEM((n_rows, width), bf16),
            pltpu.VMEM((n_cent, width), bf16),
            pltpu.VMEM((n_cent, width), bf16),
            pltpu.VMEM((n_cent, LANES), f32),
            pltpu.VMEM((n_cent, n_rows), bf16),
            pltpu.VMEM((n_cent, LANES), f32),
            *[pltpu.VMEM((n_cent, n), f32) for _ in range(n_chunks)],
            pltpu.VMEM((2, half, fb), f32),
            pltpu.VMEM((2, dp_n, half, fb), f32),
            pltpu.VMEM((2, dp_n, half, fb), bf16),
            pltpu.VMEM((2, dp_n, half, fb), bf16),
            pltpu.VMEM((2, dp_n - 1, half, fb), bf16),
            pltpu.VMEM((2, dp_n - 1, half, fb), bf16),
            pltpu.VMEM((n_chunks, 2, n), f32),
            pltpu.VMEM((n_chunks, cent_n - 1, 2, n), f32),
            pltpu.VMEM((1, n_cent), f32),
            pltpu.VMEM((group, 1, n_cent), f32),
            dma((n_chunks,)), dma((n_cent // tile,)),
            dma((2, dp_n)), dma((2, dp_n)),
            dma((2, dp_n - 1)), dma((2, dp_n - 1)),
            dma((n_chunks, cent_n - 1)), dma((n_chunks, cent_n - 1)),
            dma((group,)), dma((group,)),
        ],
        compiler_params=pltpu.CompilerParams(
            collective_id=0, has_side_effects=True, vmem_limit_bytes=56 * 1024 * 1024),
    )(rows, panel, scales.T, inv_temp)
    sums, counts = pl.pallas_call(
        place,
        out_shape=(jax.ShapeDtypeStruct((fb, n_cent), f32), jax.ShapeDtypeStruct((1, n_cent), f32)),
        in_specs=[pl.BlockSpec(memory_space=pltpu.VMEM)] * 2,
        out_specs=(pl.BlockSpec(memory_space=pltpu.VMEM),) * 2,
    )(sums, counts)
    return sums, counts.reshape(n_cent)


def solution(mesh):
    sizes = (mesh.shape["dp"], mesh.shape["cent"], mesh.shape["rep"])
    in_specs = (P(("dp", "rep"), None), P("cent", None), P("cent", None), P())
    out_specs = (P(("dp", "rep"), "cent"), P("cent"))
    return jax.shard_map(
        functools.partial(on_device, sizes), mesh=mesh, in_specs=in_specs, out_specs=out_specs,
        check_vma=False,
    )
```

```python
import functools
import math

import jax
import jax.numpy as jnp
from jax import lax
from jax.experimental import pallas as pl
from jax.experimental.pallas import tpu as pltpu
from jax.sharding import PartitionSpec as P

MESH = pl.DeviceIdType.MESH
NT = (((1,), (1,)), ((), ()))
NN = (((1,), (0,)), ((), ()))
LANES = 128


def flip(index, mask, bits):
    for b in range(bits):
        if (mask >> b) & 1:
            index = index + (1 << b) - (2 << b) * ((index // (1 << b)) % 2)
    return index


def first_step(q, order):
    for j, b in enumerate(order):
        if (q >> b) & 1:
            return j
    return len(order)


def kernel(dp_n, cent_n, rep_n, parts,
           rows_hbm, panel_hbm, scales_ref, temp_ref,
           out_ref, counts_ref, *scratch):
    n_chunks, tile = parts
    scratch = list(scratch)
    rows_ref, panel_ref, cent_ref, bias_ref, w_ref, cnt_ref = scratch[:6]
    t_refs = scratch[6:6 + n_chunks]
    (early_ref, own_ref, core_out, core_in, dp_out, dp_in, stat_out, stat_in, cnt_out, cnt_in,
     rows_sem, panel_sem, core_ss, core_rs, dp_ss, dp_rs, stat_ss, stat_rs,
     cnt_ss, cnt_rs) = scratch[6 + n_chunks:]

    n_rows, width = rows_ref.shape
    n_cent = cent_ref.shape[0]
    n = n_rows // n_chunks
    n_blk = scales_ref.shape[0]
    blk = width // n_blk
    fb = out_ref.shape[1]
    half = n_cent // 2
    bits = dp_n.bit_length() - 1

    d = lax.axis_index("dp")
    z = lax.axis_index("cent")
    r = lax.axis_index("rep")

    first_rows = pltpu.make_async_copy(
        rows_hbm.at[pl.ds(0, n)], rows_ref.at[pl.ds(0, n)], rows_sem.at[0])
    panel_copies = []
    for i, k in enumerate(range(0, n_cent, tile)):
        cp = pltpu.make_async_copy(
            panel_hbm.at[pl.ds(k, tile)], panel_ref.at[pl.ds(k, tile)], panel_sem.at[i])
        cp.start()
        panel_copies.append(cp)
        if i == 0:
            first_rows.start()
    row_copies = [first_rows]
    for c in range(1, n_chunks):
        cp = pltpu.make_async_copy(
            rows_hbm.at[pl.ds(c * n, n)], rows_ref.at[pl.ds(c * n, n)], rows_sem.at[c])
        cp.start()
        row_copies.append(cp)

    z_peers = [lax.rem(z + o, cent_n) for o in range(1, cent_n)]
    group = [(lax.rem(d + o // rep_n, dp_n), lax.rem(r + o % rep_n, rep_n))
             for o in range(1, dp_n * rep_n)]
    barrier = pltpu.get_barrier_semaphore()
    for peer in z_peers:
        pl.semaphore_signal(barrier, inc=1, device_id={"cent": peer}, device_id_type=MESH)
    for pd, pr in group:
        pl.semaphore_signal(barrier, inc=1, device_id={"dp": pd, "rep": pr}, device_id_type=MESH)

    scale2 = temp_ref[0].astype(jnp.float32) * (math.log2(math.e) / math.sqrt(width))

    scales = scales_ref[...].T

    def centroids_tile(k):
        panel_copies[k // tile].wait()
        sq = jnp.zeros((tile, blk), jnp.float32)
        for b in range(n_blk):
            full = panel_ref[k:k + tile, b * blk:(b + 1) * blk].astype(jnp.float32)
            full = (full * scales[k:k + tile, b:b + 1]).astype(jnp.bfloat16)
            cent_ref[k:k + tile, b * blk:(b + 1) * blk] = full
            wide = full.astype(jnp.float32)
            sq = sq + wide * wide
        norm = jnp.sum(sq, axis=1, keepdims=True)
        bias_ref[k:k + tile, :] = jnp.broadcast_to((-0.5 * scale2) * norm, (tile, LANES))

    stat_copies = []

    def logits_tile(c, k):
        prod = lax.dot_general(cent_ref[k:k + tile, :], rows_ref[c * n:(c + 1) * n, :], NT,
                               preferred_element_type=jnp.float32)
        bias = jnp.concatenate([bias_ref[k:k + tile, :]] * (n // LANES), axis=1)
        t = prod * scale2 + bias
        t_refs[c][k:k + tile, :] = t
        return jnp.max(t.reshape(tile // 8, 8, n), axis=0)

    def exp_tile(c, k, top):
        e = jnp.exp2(t_refs[c][k:k + tile, :] - top)
        t_refs[c][k:k + tile, :] = e
        return jnp.sum(e.reshape(tile // 8, 8, n), axis=0)

    def send_stats(c, top, total):
        stat_out[c, 0:1, :] = top
        stat_out[c, 1:2, :] = total
        for o, peer in enumerate(z_peers):
            cp = pltpu.make_async_remote_copy(
                stat_out.at[c], stat_in.at[c, o], stat_ss.at[c, o], stat_rs.at[c, o],
                device_id={"cent": peer}, device_id_type=MESH)
            cp.start()
            stat_copies.append(cp)

    def ratios(c):
        for cp in stat_copies[c * len(z_peers):(c + 1) * len(z_peers)]:
            cp.wait_recv()
        mine = stat_out[c, 0:1, :]
        top = mine
        for o in range(len(z_peers)):
            top = jnp.maximum(top, stat_in[c, o, 0:1, :])
        total = stat_out[c, 1:2, :] * jnp.exp2(mine - top)
        for o in range(len(z_peers)):
            total = total + stat_in[c, o, 1:2, :] * jnp.exp2(stat_in[c, o, 0:1, :] - top)
        return jnp.exp2(mine - top) / total

    def weights_tile(c, k, ratio):
        w = t_refs[c][k:k + tile, :] * ratio
        w_ref[k:k + tile, c * n:(c + 1) * n] = w.astype(jnp.bfloat16)
        part = w[:, :LANES]
        for l in range(LANES, n, LANES):
            part = part + w[:, l:l + LANES]
        if c > 0:
            part = part + cnt_ref[k:k + tile, :]
        cnt_ref[k:k + tile, :] = part

    def weights(c, ratio):
        for k in range(0, n_cent, tile):
            weights_tile(c, k, ratio)

    tops = []
    centroids_tile(0)
    for c in range(n_chunks + 1):
        if c < n_chunks:
            row_copies[c].wait()
        if c >= 3:
            ratio = ratios(c - 3)
        best = total = None
        for k in range(0, n_cent, tile):
            if c == 0 and k + tile < n_cent:
                centroids_tile(k + tile)
            if c < n_chunks:
                m = logits_tile(c, k)
                best = m if best is None else jnp.maximum(best, m)
            if c > 0:
                part = exp_tile(c - 1, k, tops[c - 1])
                total = part if total is None else total + part
            if c >= 3:
                weights_tile(c - 3, k, ratio)
        if c < n_chunks:
            tops.append(jnp.max(best, axis=0, keepdims=True))
        if c == 1:
            pl.semaphore_wait(barrier, len(z_peers) + len(group))
        if c > 0:
            send_stats(c - 1, tops[c - 1], jnp.sum(total, axis=0, keepdims=True))

    def columns(q):
        return pl.ds(pl.multiple_of(flip(d, q, bits) * (2 * fb), 2 * fb), 2 * fb)

    core_copies = {}
    dp_copies = {}

    first = r == 0
    orders = [list(range(bits)), list(range(bits))[::-1]]

    def dot(start, stop, h, q):
        return lax.dot_general(w_ref[h * half:(h + 1) * half, start:stop],
                               rows_ref[start:stop, columns(q)], NN,
                               preferred_element_type=jnp.float32)

    def split(h, q, prod):
        own_ref[h, q] = jnp.where(first, prod[:, :fb], prod[:, fb:])
        core_out[h, q] = jnp.where(first, prod[:, fb:], prod[:, :fb]).astype(jnp.bfloat16)
        cp = pltpu.make_async_remote_copy(
            core_out.at[h, q], core_in.at[h, q], core_ss.at[h, q], core_rs.at[h, q],
            device_id={"rep": 1 - r}, device_id_type=MESH)
        cp.start()
        core_copies[h, q] = cp

    def finish(h, q):
        order = orders[h]
        j = first_step(q, order)
        core_copies[h, q].wait_recv()
        total = own_ref[h, q] + core_in[h, q].astype(jnp.float32)
        for i in range(j):
            src = q ^ (1 << order[i])
            dp_copies[h, src].wait_recv()
            total = total + dp_in[h, src - 1].astype(jnp.float32)
        if q == 0:
            out_ref[h * half:(h + 1) * half, :] = total
            return
        dp_out[h, q - 1] = total.astype(jnp.bfloat16)
        cp = pltpu.make_async_remote_copy(
            dp_out.at[h, q - 1], dp_in.at[h, q - 1], dp_ss.at[h, q - 1], dp_rs.at[h, q - 1],
            device_id={"dp": flip(d, 1 << order[j], bits)}, device_id_type=MESH)
        cp.start()
        dp_copies[h, q] = cp

    ranked = [sorted(range(dp_n), reverse=True, key=lambda q: [(q >> b) & 1 for b in order])
              for order in orders]

    q0 = ranked[0][0]
    known = n_chunks - 2
    steps = [(0, known * n)] + [(c * n, (c + 1) * n) for c in range(known, n_chunks)]
    for i, (start, stop) in enumerate(steps):
        if i > 0:
            c = known + i - 1
            weights(c, ratios(c))
        for h in range(2):
            prod = dot(start, stop, h, q0)
            if i > 0:
                prod = prod + early_ref[h]
            if i < len(steps) - 1:
                early_ref[h] = prod
            else:
                split(h, q0, prod)

    cnt_out[...] = jnp.sum(cnt_ref[...].T, axis=0, keepdims=True)
    cnt_copies = []
    for o, (pd, pr) in enumerate(group):
        cp = pltpu.make_async_remote_copy(
            cnt_out, cnt_in.at[o], cnt_ss.at[o], cnt_rs.at[o],
            device_id={"dp": pd, "rep": pr}, device_id_type=MESH)
        cp.start()
        cnt_copies.append(cp)

    for i in range(1, dp_n):
        for h in range(2):
            split(h, ranked[0][i], dot(0, n_rows, h, ranked[0][i]))
            if first_step(ranked[0][i - 1], orders[h]) == 0:
                finish(h, ranked[0][i - 1])
    later = [(first_step(q, orders[h]), i, h, q) for h in range(2)
             for i, q in enumerate(ranked[h]) if first_step(q, orders[h]) > 0]
    later.sort()
    for _, _, h, q in later[:-2]:
        finish(h, q)

    counts = cnt_out[...]
    for o, cp in enumerate(cnt_copies):
        cp.wait_recv()
        counts = counts + cnt_in[o]
    counts_ref[...] = counts

    for _, _, h, q in later[-2:]:
        finish(h, q)

    for cp in stat_copies + cnt_copies + list(core_copies.values()) + list(dp_copies.values()):
        cp.wait_send()


def place(sums_ref, counts_in, out_ref, counts_ref):
    out_ref[...] = sums_ref[...].T
    counts_ref[...] = counts_in[...]


def on_device(sizes, rows, panel, scales, inv_temp):
    dp_n, cent_n, rep_n = sizes
    n_rows, width = rows.shape
    n_cent = panel.shape[0]
    n_chunks = 4
    tile = 256
    n = n_rows // n_chunks
    fb = width // (dp_n * rep_n)
    half = n_cent // 2
    group = dp_n * rep_n - 1
    f32, bf16 = jnp.float32, jnp.bfloat16
    dma = pltpu.SemaphoreType.DMA
    body = functools.partial(kernel, dp_n, cent_n, rep_n, (n_chunks, tile))
    sums, counts = pl.pallas_call(
        body,
        out_shape=(jax.ShapeDtypeStruct((n_cent, fb), f32), jax.ShapeDtypeStruct((1, n_cent), f32)),
        in_specs=[pl.BlockSpec(memory_space=pl.ANY), pl.BlockSpec(memory_space=pl.ANY),
                  pl.BlockSpec(memory_space=pltpu.VMEM), pl.BlockSpec(memory_space=pltpu.SMEM)],
        out_specs=(pl.BlockSpec(memory_space=pltpu.VMEM), pl.BlockSpec(memory_space=pltpu.VMEM)),
        scratch_shapes=[
            pltpu.VMEM((n_rows, width), bf16),
            pltpu.VMEM((n_cent, width), bf16),
            pltpu.VMEM((n_cent, width), bf16),
            pltpu.VMEM((n_cent, LANES), f32),
            pltpu.VMEM((n_cent, n_rows), bf16),
            pltpu.VMEM((n_cent, LANES), f32),
            *[pltpu.VMEM((n_cent, n), f32) for _ in range(n_chunks)],
            pltpu.VMEM((2, half, 2 * fb), f32),
            pltpu.VMEM((2, dp_n, half, fb), f32),
            pltpu.VMEM((2, dp_n, half, fb), bf16),
            pltpu.VMEM((2, dp_n, half, fb), bf16),
            pltpu.VMEM((2, dp_n - 1, half, fb), bf16),
            pltpu.VMEM((2, dp_n - 1, half, fb), bf16),
            pltpu.VMEM((n_chunks, 2, n), f32),
            pltpu.VMEM((n_chunks, cent_n - 1, 2, n), f32),
            pltpu.VMEM((1, n_cent), f32),
            pltpu.VMEM((group, 1, n_cent), f32),
            dma((n_chunks,)), dma((n_cent // tile,)),
            dma((2, dp_n)), dma((2, dp_n)),
            dma((2, dp_n - 1)), dma((2, dp_n - 1)),
            dma((n_chunks, cent_n - 1)), dma((n_chunks, cent_n - 1)),
            dma((group,)), dma((group,)),
        ],
        compiler_params=pltpu.CompilerParams(
            collective_id=0, has_side_effects=True, vmem_limit_bytes=56 * 1024 * 1024),
    )(rows, panel, scales.T, inv_temp)
    sums, counts = pl.pallas_call(
        place,
        out_shape=(jax.ShapeDtypeStruct((fb, n_cent), f32), jax.ShapeDtypeStruct((1, n_cent), f32)),
        in_specs=[pl.BlockSpec(memory_space=pltpu.VMEM)] * 2,
        out_specs=(pl.BlockSpec(memory_space=pltpu.VMEM),) * 2,
    )(sums, counts)
    return sums, counts.reshape(n_cent)


def solution(mesh):
    sizes = (mesh.shape["dp"], mesh.shape["cent"], mesh.shape["rep"])
    in_specs = (P(("dp", "rep"), None), P("cent", None), P("cent", None), P())
    out_specs = (P(("dp", "rep"), "cent"), P("cent"))
    return jax.shard_map(
        functools.partial(on_device, sizes), mesh=mesh, in_specs=in_specs, out_specs=out_specs,
        check_vma=False,
    )
```

```python
import functools
import math

import jax
import jax.numpy as jnp
from jax import lax
from jax.experimental import pallas as pl
from jax.experimental.pallas import tpu as pltpu
from jax.sharding import PartitionSpec as P

MESH = pl.DeviceIdType.MESH
NT = (((1,), (1,)), ((), ()))
NN = (((1,), (0,)), ((), ()))
LANES = 128


def flip(index, mask, bits):
    for b in range(bits):
        if (mask >> b) & 1:
            index = index + (1 << b) - (2 << b) * ((index // (1 << b)) % 2)
    return index


def first_step(q, order):
    for j, b in enumerate(order):
        if (q >> b) & 1:
            return j
    return len(order)


def kernel(dp_n, cent_n, rep_n, parts,
           rows_hbm, panel_hbm, scales_ref, temp_ref,
           out_ref, counts_ref, *scratch):
    n_chunks, tile = parts
    scratch = list(scratch)
    rows_ref, panel_ref, cent_ref, bias_ref, w_ref, cnt_ref, scales_t = scratch[:7]
    t_refs = scratch[7:7 + n_chunks]
    (early_ref, own_ref, core_out, core_in, dp_out, dp_in, stat_out, stat_in, cnt_out, cnt_in,
     rows_sem, panel_sem, core_ss, core_rs, dp_ss, dp_rs, stat_ss, stat_rs,
     cnt_ss, cnt_rs) = scratch[7 + n_chunks:]

    n_rows, width = rows_ref.shape
    n_cent = cent_ref.shape[0]
    n = n_rows // n_chunks
    n_blk = scales_ref.shape[0]
    blk = width // n_blk
    fb = out_ref.shape[1]
    half = n_cent // 2
    bits = dp_n.bit_length() - 1

    d = lax.axis_index("dp")
    z = lax.axis_index("cent")
    r = lax.axis_index("rep")

    first_rows = pltpu.make_async_copy(
        rows_hbm.at[pl.ds(0, n)], rows_ref.at[pl.ds(0, n)], rows_sem.at[0])
    panel_copies = []
    for i, k in enumerate(range(0, n_cent, tile)):
        cp = pltpu.make_async_copy(
            panel_hbm.at[pl.ds(k, tile)], panel_ref.at[pl.ds(k, tile)], panel_sem.at[i])
        cp.start()
        panel_copies.append(cp)
        if i == 0:
            first_rows.start()
    row_copies = [first_rows]
    for c in range(1, n_chunks):
        cp = pltpu.make_async_copy(
            rows_hbm.at[pl.ds(c * n, n)], rows_ref.at[pl.ds(c * n, n)], rows_sem.at[c])
        cp.start()
        row_copies.append(cp)

    z_peers = [lax.rem(z + o, cent_n) for o in range(1, cent_n)]
    group = [(lax.rem(d + o // rep_n, dp_n), lax.rem(r + o % rep_n, rep_n))
             for o in range(1, dp_n * rep_n)]
    barrier = pltpu.get_barrier_semaphore()
    for peer in z_peers:
        pl.semaphore_signal(barrier, inc=1, device_id={"cent": peer}, device_id_type=MESH)
    for pd, pr in group:
        pl.semaphore_signal(barrier, inc=1, device_id={"dp": pd, "rep": pr}, device_id_type=MESH)

    scale2 = temp_ref[0].astype(jnp.float32) * (math.log2(math.e) / math.sqrt(width))

    scales = scales_ref[...].T

    scales_t[:, :n_blk] = scales
    for cp in panel_copies:
        cp.wait()

    def at(i):
        return pl.ds(pl.multiple_of(i * tile, tile), tile)

    def each_tile(body, init=0):
        return lax.fori_loop(0, n_cent // tile, body, init)

    def centroids_tile(i, carry):
        sq = jnp.zeros((tile, blk), jnp.float32)
        for b in range(n_blk):
            full = panel_ref[at(i), b * blk:(b + 1) * blk].astype(jnp.float32)
            full = (full * scales_t[at(i), b:b + 1]).astype(jnp.bfloat16)
            cent_ref[at(i), b * blk:(b + 1) * blk] = full
            wide = full.astype(jnp.float32)
            sq = sq + wide * wide
        norm = jnp.sum(sq, axis=1, keepdims=True)
        bias_ref[at(i), :] = jnp.broadcast_to((-0.5 * scale2) * norm, (tile, LANES))
        return carry

    each_tile(centroids_tile)

    stat_copies = []

    def logits_tile(c, i):
        prod = lax.dot_general(cent_ref[at(i), :], rows_ref[c * n:(c + 1) * n, :], NT,
                               preferred_element_type=jnp.float32)
        bias = jnp.concatenate([bias_ref[at(i), :]] * (n // LANES), axis=1)
        t = prod * scale2 + bias
        t_refs[c][at(i), :] = t
        return jnp.max(t.reshape(tile // 8, 8, n), axis=0)

    def exp_tile(c, i, top):
        e = jnp.exp2(t_refs[c][at(i), :] - top)
        t_refs[c][at(i), :] = e
        return jnp.sum(e.reshape(tile // 8, 8, n), axis=0)

    def send_stats(c, top, total):
        stat_out[c, 0:1, :] = top
        stat_out[c, 1:2, :] = total
        for o, peer in enumerate(z_peers):
            cp = pltpu.make_async_remote_copy(
                stat_out.at[c], stat_in.at[c, o], stat_ss.at[c, o], stat_rs.at[c, o],
                device_id={"cent": peer}, device_id_type=MESH)
            cp.start()
            stat_copies.append(cp)

    def ratios(c):
        for cp in stat_copies[c * len(z_peers):(c + 1) * len(z_peers)]:
            cp.wait_recv()
        mine = stat_out[c, 0:1, :]
        top = mine
        for o in range(len(z_peers)):
            top = jnp.maximum(top, stat_in[c, o, 0:1, :])
        total = stat_out[c, 1:2, :] * jnp.exp2(mine - top)
        for o in range(len(z_peers)):
            total = total + stat_in[c, o, 1:2, :] * jnp.exp2(stat_in[c, o, 0:1, :] - top)
        return jnp.exp2(mine - top) / total

    def weights_tile(c, i, ratio):
        w = t_refs[c][at(i), :] * ratio
        w_ref[at(i), c * n:(c + 1) * n] = w.astype(jnp.bfloat16)
        part = w[:, :LANES]
        for l in range(LANES, n, LANES):
            part = part + w[:, l:l + LANES]
        if c > 0:
            part = part + cnt_ref[at(i), :]
        cnt_ref[at(i), :] = part

    def weights(c, ratio):
        def body(i, carry):
            weights_tile(c, i, ratio)
            return carry
        each_tile(body)

    tops = []
    for c in range(n_chunks + 1):
        if c < n_chunks:
            row_copies[c].wait()
        ratio = ratios(c - 3) if c >= 3 else None

        def body(i, carry, c=c, ratio=ratio):
            best, total = carry
            if c < n_chunks:
                best = jnp.maximum(best, logits_tile(c, i))
            if c > 0:
                total = total + exp_tile(c - 1, i, tops[c - 1])
            if c >= 3:
                weights_tile(c - 3, i, ratio)
            return best, total

        best, total = each_tile(
            body, (jnp.full((8, n), -jnp.inf, jnp.float32), jnp.zeros((8, n), jnp.float32)))
        if c < n_chunks:
            tops.append(jnp.max(best, axis=0, keepdims=True))
        if c == 1:
            pl.semaphore_wait(barrier, len(z_peers) + len(group))
        if c > 0:
            send_stats(c - 1, tops[c - 1], jnp.sum(total, axis=0, keepdims=True))

    def columns(q):
        return pl.ds(pl.multiple_of(flip(d, q, bits) * (2 * fb), 2 * fb), 2 * fb)

    core_copies = {}
    dp_copies = {}

    first = r == 0
    orders = [list(range(bits)), list(range(bits))[::-1]]

    def dot(start, stop, h, q, last, add):
        def body(i, carry):
            at_i = pl.ds(pl.multiple_of(i * tile, tile), tile)
            at_w = pl.ds(pl.multiple_of(h * half + i * tile, tile), tile)
            prod = lax.dot_general(w_ref[at_w, start:stop], rows_ref[start:stop, columns(q)], NN,
                                   preferred_element_type=jnp.float32)
            if add:
                prod = prod + early_ref[h, at_i, :]
            if not last:
                early_ref[h, at_i, :] = prod
            else:
                own_ref[h, q, at_i, :] = jnp.where(first, prod[:, :fb], prod[:, fb:])
                core_out[h, q, at_i, :] = jnp.where(
                    first, prod[:, fb:], prod[:, :fb]).astype(jnp.bfloat16)
            return carry

        lax.fori_loop(0, half // tile, body, 0)
        if last:
            cp = pltpu.make_async_remote_copy(
                core_out.at[h, q], core_in.at[h, q], core_ss.at[h, q], core_rs.at[h, q],
                device_id={"rep": 1 - r}, device_id_type=MESH)
            cp.start()
            core_copies[h, q] = cp

    def finish(h, q):
        order = orders[h]
        j = first_step(q, order)
        core_copies[h, q].wait_recv()
        total = own_ref[h, q] + core_in[h, q].astype(jnp.float32)
        for i in range(j):
            src = q ^ (1 << order[i])
            dp_copies[h, src].wait_recv()
            total = total + dp_in[h, src - 1].astype(jnp.float32)
        if q == 0:
            out_ref[h * half:(h + 1) * half, :] = total
            return
        dp_out[h, q - 1] = total.astype(jnp.bfloat16)
        cp = pltpu.make_async_remote_copy(
            dp_out.at[h, q - 1], dp_in.at[h, q - 1], dp_ss.at[h, q - 1], dp_rs.at[h, q - 1],
            device_id={"dp": flip(d, 1 << order[j], bits)}, device_id_type=MESH)
        cp.start()
        dp_copies[h, q] = cp

    ranked = [sorted(range(dp_n), reverse=True, key=lambda q: [(q >> b) & 1 for b in order])
              for order in orders]

    q0 = ranked[0][0]
    known = n_chunks - 2
    steps = [(0, known * n)] + [(c * n, (c + 1) * n) for c in range(known, n_chunks)]
    for i, (start, stop) in enumerate(steps):
        if i > 0:
            c = known + i - 1
            weights(c, ratios(c))
        for h in range(2):
            dot(start, stop, h, q0, i == len(steps) - 1, i > 0)

    cnt_out[...] = jnp.sum(cnt_ref[...].T, axis=0, keepdims=True)
    cnt_copies = []
    for o, (pd, pr) in enumerate(group):
        cp = pltpu.make_async_remote_copy(
            cnt_out, cnt_in.at[o], cnt_ss.at[o], cnt_rs.at[o],
            device_id={"dp": pd, "rep": pr}, device_id_type=MESH)
        cp.start()
        cnt_copies.append(cp)

    for i in range(1, dp_n):
        for h in range(2):
            dot(0, n_rows, h, ranked[0][i], True, False)
            if first_step(ranked[0][i - 1], orders[h]) == 0:
                finish(h, ranked[0][i - 1])
    later = [(first_step(q, orders[h]), i, h, q) for h in range(2)
             for i, q in enumerate(ranked[h]) if first_step(q, orders[h]) > 0]
    later.sort()
    for _, _, h, q in later[:-2]:
        finish(h, q)

    counts = cnt_out[...]
    for o, cp in enumerate(cnt_copies):
        cp.wait_recv()
        counts = counts + cnt_in[o]
    counts_ref[...] = counts

    for _, _, h, q in later[-2:]:
        finish(h, q)

    for cp in stat_copies + cnt_copies + list(core_copies.values()) + list(dp_copies.values()):
        cp.wait_send()


def place(sums_ref, counts_in, out_ref, counts_ref):
    out_ref[...] = sums_ref[...].T
    counts_ref[...] = counts_in[...]


def on_device(sizes, rows, panel, scales, inv_temp):
    dp_n, cent_n, rep_n = sizes
    n_rows, width = rows.shape
    n_cent = panel.shape[0]
    n_chunks = 4
    tile = 256
    n = n_rows // n_chunks
    fb = width // (dp_n * rep_n)
    half = n_cent // 2
    group = dp_n * rep_n - 1
    f32, bf16 = jnp.float32, jnp.bfloat16
    dma = pltpu.SemaphoreType.DMA
    body = functools.partial(kernel, dp_n, cent_n, rep_n, (n_chunks, tile))
    sums, counts = pl.pallas_call(
        body,
        out_shape=(jax.ShapeDtypeStruct((n_cent, fb), f32), jax.ShapeDtypeStruct((1, n_cent), f32)),
        in_specs=[pl.BlockSpec(memory_space=pl.ANY), pl.BlockSpec(memory_space=pl.ANY),
                  pl.BlockSpec(memory_space=pltpu.VMEM), pl.BlockSpec(memory_space=pltpu.SMEM)],
        out_specs=(pl.BlockSpec(memory_space=pltpu.VMEM), pl.BlockSpec(memory_space=pltpu.VMEM)),
        scratch_shapes=[
            pltpu.VMEM((n_rows, width), bf16),
            pltpu.VMEM((n_cent, width), bf16),
            pltpu.VMEM((n_cent, width), bf16),
            pltpu.VMEM((n_cent, LANES), f32),
            pltpu.VMEM((n_cent, n_rows), bf16),
            pltpu.VMEM((n_cent, LANES), f32),
            pltpu.VMEM((n_cent, LANES), f32),
            *[pltpu.VMEM((n_cent, n), f32) for _ in range(n_chunks)],
            pltpu.VMEM((2, half, 2 * fb), f32),
            pltpu.VMEM((2, dp_n, half, fb), f32),
            pltpu.VMEM((2, dp_n, half, fb), bf16),
            pltpu.VMEM((2, dp_n, half, fb), bf16),
            pltpu.VMEM((2, dp_n - 1, half, fb), bf16),
            pltpu.VMEM((2, dp_n - 1, half, fb), bf16),
            pltpu.VMEM((n_chunks, 2, n), f32),
            pltpu.VMEM((n_chunks, cent_n - 1, 2, n), f32),
            pltpu.VMEM((1, n_cent), f32),
            pltpu.VMEM((group, 1, n_cent), f32),
            dma((n_chunks,)), dma((n_cent // tile,)),
            dma((2, dp_n)), dma((2, dp_n)),
            dma((2, dp_n - 1)), dma((2, dp_n - 1)),
            dma((n_chunks, cent_n - 1)), dma((n_chunks, cent_n - 1)),
            dma((group,)), dma((group,)),
        ],
        compiler_params=pltpu.CompilerParams(
            collective_id=0, has_side_effects=True, vmem_limit_bytes=56 * 1024 * 1024),
    )(rows, panel, scales.T, inv_temp)
    sums, counts = pl.pallas_call(
        place,
        out_shape=(jax.ShapeDtypeStruct((fb, n_cent), f32), jax.ShapeDtypeStruct((1, n_cent), f32)),
        in_specs=[pl.BlockSpec(memory_space=pltpu.VMEM)] * 2,
        out_specs=(pl.BlockSpec(memory_space=pltpu.VMEM),) * 2,
    )(sums, counts)
    return sums, counts.reshape(n_cent)


def solution(mesh):
    sizes = (mesh.shape["dp"], mesh.shape["cent"], mesh.shape["rep"])
    in_specs = (P(("dp", "rep"), None), P("cent", None), P("cent", None), P())
    out_specs = (P(("dp", "rep"), "cent"), P("cent"))
    return jax.shard_map(
        functools.partial(on_device, sizes), mesh=mesh, in_specs=in_specs, out_specs=out_specs,
        check_vma=False,
    )
```

```python
import functools
import math

import jax
import jax.numpy as jnp
from jax import lax
from jax.experimental import pallas as pl
from jax.experimental.pallas import tpu as pltpu
from jax.sharding import PartitionSpec as P

MESH = pl.DeviceIdType.MESH
NT = (((1,), (1,)), ((), ()))
NN = (((1,), (0,)), ((), ()))
LANES = 128


def flip(index, mask, bits):
    for b in range(bits):
        if (mask >> b) & 1:
            index = index + (1 << b) - (2 << b) * ((index // (1 << b)) % 2)
    return index


def first_step(q, order):
    for j, b in enumerate(order):
        if (q >> b) & 1:
            return j
    return len(order)


def kernel(dp_n, cent_n, rep_n, parts,
           rows_hbm, panel_hbm, scales_ref, temp_ref,
           out_ref, counts_ref, *scratch):
    n_chunks, tile = parts
    scratch = list(scratch)
    rows_ref, panel_ref, cent_ref, bias_ref, w_ref, cnt_ref = scratch[:6]
    t_refs = scratch[6:6 + n_chunks]
    (early_ref, own_ref, core_out, core_in, dp_out, dp_in, stat_out, stat_in, cnt_out, cnt_in,
     rows_sem, panel_sem, core_ss, core_rs, dp_ss, dp_rs, stat_ss, stat_rs,
     cnt_ss, cnt_rs) = scratch[6 + n_chunks:]

    n_rows, width = rows_ref.shape
    n_cent = cent_ref.shape[0]
    n = n_rows // n_chunks
    n_blk = scales_ref.shape[0]
    blk = width // n_blk
    fb = out_ref.shape[1]
    half = n_cent // 2
    bits = dp_n.bit_length() - 1

    d = lax.axis_index("dp")
    z = lax.axis_index("cent")
    r = lax.axis_index("rep")

    first_rows = pltpu.make_async_copy(
        rows_hbm.at[pl.ds(0, n)], rows_ref.at[pl.ds(0, n)], rows_sem.at[0])
    panel_copies = []
    for i, k in enumerate(range(0, n_cent, tile)):
        cp = pltpu.make_async_copy(
            panel_hbm.at[pl.ds(k, tile)], panel_ref.at[pl.ds(k, tile)], panel_sem.at[i])
        cp.start()
        panel_copies.append(cp)
        if i == 0:
            first_rows.start()
    row_copies = [first_rows]
    for c in range(1, n_chunks):
        cp = pltpu.make_async_copy(
            rows_hbm.at[pl.ds(c * n, n)], rows_ref.at[pl.ds(c * n, n)], rows_sem.at[c])
        cp.start()
        row_copies.append(cp)

    z_peers = [lax.rem(z + o, cent_n) for o in range(1, cent_n)]
    group = [(lax.rem(d + o // rep_n, dp_n), lax.rem(r + o % rep_n, rep_n))
             for o in range(1, dp_n * rep_n)]
    barrier = pltpu.get_barrier_semaphore()
    for peer in z_peers:
        pl.semaphore_signal(barrier, inc=1, device_id={"cent": peer}, device_id_type=MESH)
    for pd, pr in group:
        pl.semaphore_signal(barrier, inc=1, device_id={"dp": pd, "rep": pr}, device_id_type=MESH)

    scale2 = temp_ref[0].astype(jnp.float32) * (math.log2(math.e) / math.sqrt(width))

    scales = scales_ref[...].T

    def centroids_tile(k):
        panel_copies[k // tile].wait()
        sq = jnp.zeros((tile, blk), jnp.float32)
        for b in range(n_blk):
            full = panel_ref[k:k + tile, b * blk:(b + 1) * blk].astype(jnp.float32)
            full = (full * scales[k:k + tile, b:b + 1]).astype(jnp.bfloat16)
            cent_ref[k:k + tile, b * blk:(b + 1) * blk] = full
            wide = full.astype(jnp.float32)
            sq = sq + wide * wide
        norm = jnp.sum(sq, axis=1, keepdims=True)
        bias_ref[k:k + tile, :] = jnp.broadcast_to((-0.5 * scale2) * norm, (tile, LANES))

    stat_copies = []

    tall, wide_n = 2 * tile, n // 2

    def logits_tile(c, k, col):
        prod = lax.dot_general(cent_ref[k:k + tall, :],
                               rows_ref[c * n + col:c * n + col + wide_n, :], NT,
                               preferred_element_type=jnp.float32)
        bias = jnp.concatenate([bias_ref[k:k + tall, :]] * (wide_n // LANES), axis=1)
        t = prod * scale2 + bias
        t_refs[c][k:k + tall, col:col + wide_n] = t
        return jnp.max(t.reshape(tall // 8, 8, wide_n), axis=0)

    def exp_tile(c, k, top):
        e = jnp.exp2(t_refs[c][k:k + tile, :] - top)
        t_refs[c][k:k + tile, :] = e
        return jnp.sum(e.reshape(tile // 8, 8, n), axis=0)

    def send_stats(c, top, total):
        stat_out[c, 0:1, :] = top
        stat_out[c, 1:2, :] = total
        for o, peer in enumerate(z_peers):
            cp = pltpu.make_async_remote_copy(
                stat_out.at[c], stat_in.at[c, o], stat_ss.at[c, o], stat_rs.at[c, o],
                device_id={"cent": peer}, device_id_type=MESH)
            cp.start()
            stat_copies.append(cp)

    def ratios(c):
        for cp in stat_copies[c * len(z_peers):(c + 1) * len(z_peers)]:
            cp.wait_recv()
        mine = stat_out[c, 0:1, :]
        top = mine
        for o in range(len(z_peers)):
            top = jnp.maximum(top, stat_in[c, o, 0:1, :])
        total = stat_out[c, 1:2, :] * jnp.exp2(mine - top)
        for o in range(len(z_peers)):
            total = total + stat_in[c, o, 1:2, :] * jnp.exp2(stat_in[c, o, 0:1, :] - top)
        return jnp.exp2(mine - top) / total

    def weights_tile(c, k, ratio):
        w = t_refs[c][k:k + tile, :] * ratio
        w_ref[k:k + tile, c * n:(c + 1) * n] = w.astype(jnp.bfloat16)
        part = w[:, :LANES]
        for l in range(LANES, n, LANES):
            part = part + w[:, l:l + LANES]
        if c > 0:
            part = part + cnt_ref[k:k + tile, :]
        cnt_ref[k:k + tile, :] = part

    def weights(c, ratio):
        for k in range(0, n_cent, tile):
            weights_tile(c, k, ratio)

    tops = []
    for k in range(0, tall, tile):
        centroids_tile(k)
    for c in range(n_chunks + 1):
        if c < n_chunks:
            row_copies[c].wait()
        if c >= 3:
            ratio = ratios(c - 3)
        best, total = [None, None], None
        for k in range(0, n_cent, tall):
            for j in range(2):
                sub = k + j * tile
                if c == 0 and sub + tall < n_cent:
                    centroids_tile(sub + tall)
                if c < n_chunks:
                    m = logits_tile(c, k, j * wide_n)
                    best[j] = m if best[j] is None else jnp.maximum(best[j], m)
                if c > 0:
                    part = exp_tile(c - 1, sub, tops[c - 1])
                    total = part if total is None else total + part
                if c >= 3:
                    weights_tile(c - 3, sub, ratio)
        if c < n_chunks:
            tops.append(jnp.max(jnp.concatenate(best, axis=1), axis=0, keepdims=True))
        if c == 1:
            pl.semaphore_wait(barrier, len(z_peers) + len(group))
        if c > 0:
            send_stats(c - 1, tops[c - 1], jnp.sum(total, axis=0, keepdims=True))

    def columns(q):
        return pl.ds(pl.multiple_of(flip(d, q, bits) * (2 * fb), 2 * fb), 2 * fb)

    core_copies = {}
    dp_copies = {}

    first = r == 0
    orders = [list(range(bits)), list(range(bits))[::-1]]

    def dot(start, stop, h, q):
        return lax.dot_general(w_ref[h * half:(h + 1) * half, start:stop],
                               rows_ref[start:stop, columns(q)], NN,
                               preferred_element_type=jnp.float32)

    def split(h, q, prod):
        own_ref[h, q] = jnp.where(first, prod[:, :fb], prod[:, fb:])
        core_out[h, q] = jnp.where(first, prod[:, fb:], prod[:, :fb]).astype(jnp.bfloat16)
        cp = pltpu.make_async_remote_copy(
            core_out.at[h, q], core_in.at[h, q], core_ss.at[h, q], core_rs.at[h, q],
            device_id={"rep": 1 - r}, device_id_type=MESH)
        cp.start()
        core_copies[h, q] = cp

    def finish(h, q):
        order = orders[h]
        j = first_step(q, order)
        core_copies[h, q].wait_recv()
        total = own_ref[h, q] + core_in[h, q].astype(jnp.float32)
        for i in range(j):
            src = q ^ (1 << order[i])
            dp_copies[h, src].wait_recv()
            total = total + dp_in[h, src - 1].astype(jnp.float32)
        if q == 0:
            out_ref[h * half:(h + 1) * half, :] = total
            return
        dp_out[h, q - 1] = total.astype(jnp.bfloat16)
        cp = pltpu.make_async_remote_copy(
            dp_out.at[h, q - 1], dp_in.at[h, q - 1], dp_ss.at[h, q - 1], dp_rs.at[h, q - 1],
            device_id={"dp": flip(d, 1 << order[j], bits)}, device_id_type=MESH)
        cp.start()
        dp_copies[h, q] = cp

    ranked = [sorted(range(dp_n), reverse=True, key=lambda q: [(q >> b) & 1 for b in order])
              for order in orders]

    q0 = ranked[0][0]
    known = n_chunks - 2
    steps = [(0, known * n)] + [(c * n, (c + 1) * n) for c in range(known, n_chunks)]
    for i, (start, stop) in enumerate(steps):
        if i > 0:
            c = known + i - 1
            weights(c, ratios(c))
        for h in range(2):
            prod = dot(start, stop, h, q0)
            if i > 0:
                prod = prod + early_ref[h]
            if i < len(steps) - 1:
                early_ref[h] = prod
            else:
                split(h, q0, prod)

    cnt_out[...] = jnp.sum(cnt_ref[...].T, axis=0, keepdims=True)
    cnt_copies = []
    for o, (pd, pr) in enumerate(group):
        cp = pltpu.make_async_remote_copy(
            cnt_out, cnt_in.at[o], cnt_ss.at[o], cnt_rs.at[o],
            device_id={"dp": pd, "rep": pr}, device_id_type=MESH)
        cp.start()
        cnt_copies.append(cp)

    for i in range(1, dp_n):
        for h in range(2):
            split(h, ranked[0][i], dot(0, n_rows, h, ranked[0][i]))
            if first_step(ranked[0][i - 1], orders[h]) == 0:
                finish(h, ranked[0][i - 1])
    later = [(first_step(q, orders[h]), i, h, q) for h in range(2)
             for i, q in enumerate(ranked[h]) if first_step(q, orders[h]) > 0]
    later.sort()
    for _, _, h, q in later[:-2]:
        finish(h, q)

    counts = cnt_out[...]
    for o, cp in enumerate(cnt_copies):
        cp.wait_recv()
        counts = counts + cnt_in[o]
    counts_ref[...] = counts

    for _, _, h, q in later[-2:]:
        finish(h, q)

    for cp in stat_copies + cnt_copies + list(core_copies.values()) + list(dp_copies.values()):
        cp.wait_send()


def place(sums_ref, counts_in, out_ref, counts_ref):
    out_ref[...] = sums_ref[...].T
    counts_ref[...] = counts_in[...]


def on_device(sizes, rows, panel, scales, inv_temp):
    dp_n, cent_n, rep_n = sizes
    n_rows, width = rows.shape
    n_cent = panel.shape[0]
    n_chunks = 4
    tile = 256
    n = n_rows // n_chunks
    fb = width // (dp_n * rep_n)
    half = n_cent // 2
    group = dp_n * rep_n - 1
    f32, bf16 = jnp.float32, jnp.bfloat16
    dma = pltpu.SemaphoreType.DMA
    body = functools.partial(kernel, dp_n, cent_n, rep_n, (n_chunks, tile))
    sums, counts = pl.pallas_call(
        body,
        out_shape=(jax.ShapeDtypeStruct((n_cent, fb), f32), jax.ShapeDtypeStruct((1, n_cent), f32)),
        in_specs=[pl.BlockSpec(memory_space=pl.ANY), pl.BlockSpec(memory_space=pl.ANY),
                  pl.BlockSpec(memory_space=pltpu.VMEM), pl.BlockSpec(memory_space=pltpu.SMEM)],
        out_specs=(pl.BlockSpec(memory_space=pltpu.VMEM), pl.BlockSpec(memory_space=pltpu.VMEM)),
        scratch_shapes=[
            pltpu.VMEM((n_rows, width), bf16),
            pltpu.VMEM((n_cent, width), bf16),
            pltpu.VMEM((n_cent, width), bf16),
            pltpu.VMEM((n_cent, LANES), f32),
            pltpu.VMEM((n_cent, n_rows), bf16),
            pltpu.VMEM((n_cent, LANES), f32),
            *[pltpu.VMEM((n_cent, n), f32) for _ in range(n_chunks)],
            pltpu.VMEM((2, half, 2 * fb), f32),
            pltpu.VMEM((2, dp_n, half, fb), f32),
            pltpu.VMEM((2, dp_n, half, fb), bf16),
            pltpu.VMEM((2, dp_n, half, fb), bf16),
            pltpu.VMEM((2, dp_n - 1, half, fb), bf16),
            pltpu.VMEM((2, dp_n - 1, half, fb), bf16),
            pltpu.VMEM((n_chunks, 2, n), f32),
            pltpu.VMEM((n_chunks, cent_n - 1, 2, n), f32),
            pltpu.VMEM((1, n_cent), f32),
            pltpu.VMEM((group, 1, n_cent), f32),
            dma((n_chunks,)), dma((n_cent // tile,)),
            dma((2, dp_n)), dma((2, dp_n)),
            dma((2, dp_n - 1)), dma((2, dp_n - 1)),
            dma((n_chunks, cent_n - 1)), dma((n_chunks, cent_n - 1)),
            dma((group,)), dma((group,)),
        ],
        compiler_params=pltpu.CompilerParams(
            collective_id=0, has_side_effects=True, vmem_limit_bytes=56 * 1024 * 1024),
    )(rows, panel, scales.T, inv_temp)
    sums, counts = pl.pallas_call(
        place,
        out_shape=(jax.ShapeDtypeStruct((fb, n_cent), f32), jax.ShapeDtypeStruct((1, n_cent), f32)),
        in_specs=[pl.BlockSpec(memory_space=pltpu.VMEM)] * 2,
        out_specs=(pl.BlockSpec(memory_space=pltpu.VMEM),) * 2,
    )(sums, counts)
    return sums, counts.reshape(n_cent)


def solution(mesh):
    sizes = (mesh.shape["dp"], mesh.shape["cent"], mesh.shape["rep"])
    in_specs = (P(("dp", "rep"), None), P("cent", None), P("cent", None), P())
    out_specs = (P(("dp", "rep"), "cent"), P("cent"))
    return jax.shard_map(
        functools.partial(on_device, sizes), mesh=mesh, in_specs=in_specs, out_specs=out_specs,
        check_vma=False,
    )
```

```python
import functools
import math

import jax
import jax.numpy as jnp
from jax import lax
from jax.experimental import pallas as pl
from jax.experimental.pallas import tpu as pltpu
from jax.sharding import PartitionSpec as P

MESH = pl.DeviceIdType.MESH
NT = (((1,), (1,)), ((), ()))
NN = (((1,), (0,)), ((), ()))
LANES = 128


def flip(index, mask, bits):
    for b in range(bits):
        if (mask >> b) & 1:
            index = index + (1 << b) - (2 << b) * ((index // (1 << b)) % 2)
    return index


def first_step(q, order):
    for j, b in enumerate(order):
        if (q >> b) & 1:
            return j
    return len(order)


def kernel(dp_n, cent_n, rep_n, parts,
           rows_hbm, panel_hbm, scales_ref, temp_ref,
           out_ref, counts_ref, *scratch):
    n_chunks, tile = parts
    scratch = list(scratch)
    rows_ref, panel_ref, cent_ref, bias_ref, w_ref, cnt_ref = scratch[:6]
    t_refs = scratch[6:6 + n_chunks]
    (early_ref, own_ref, core_out, core_in, dp_out, dp_in, stat_out, stat_in, cnt_out, cnt_in,
     rows_sem, panel_sem, core_ss, core_rs, dp_ss, dp_rs, stat_ss, stat_rs,
     cnt_ss, cnt_rs) = scratch[6 + n_chunks:]

    n_rows, width = rows_ref.shape
    n_cent = cent_ref.shape[0]
    n = n_rows // n_chunks
    n_blk = scales_ref.shape[0]
    blk = width // n_blk
    fb = out_ref.shape[1]
    half = n_cent // 2
    bits = dp_n.bit_length() - 1

    d = lax.axis_index("dp")
    z = lax.axis_index("cent")
    r = lax.axis_index("rep")

    first_rows = pltpu.make_async_copy(
        rows_hbm.at[pl.ds(0, n)], rows_ref.at[pl.ds(0, n)], rows_sem.at[0])
    panel_copies = []
    for i, k in enumerate(range(0, n_cent, tile)):
        cp = pltpu.make_async_copy(
            panel_hbm.at[pl.ds(k, tile)], panel_ref.at[pl.ds(k, tile)], panel_sem.at[i])
        cp.start()
        panel_copies.append(cp)
        if i == 0:
            first_rows.start()
    row_copies = [first_rows]
    for c in range(1, n_chunks):
        cp = pltpu.make_async_copy(
            rows_hbm.at[pl.ds(c * n, n)], rows_ref.at[pl.ds(c * n, n)], rows_sem.at[c])
        cp.start()
        row_copies.append(cp)

    z_peers = [lax.rem(z + o, cent_n) for o in range(1, cent_n)]
    group = [(lax.rem(d + o // rep_n, dp_n), lax.rem(r + o % rep_n, rep_n))
             for o in range(1, dp_n * rep_n)]
    barrier = pltpu.get_barrier_semaphore()
    for peer in z_peers:
        pl.semaphore_signal(barrier, inc=1, device_id={"cent": peer}, device_id_type=MESH)
    for pd, pr in group:
        pl.semaphore_signal(barrier, inc=1, device_id={"dp": pd, "rep": pr}, device_id_type=MESH)

    scale2 = temp_ref[0].astype(jnp.float32) * (math.log2(math.e) / math.sqrt(width))

    scales = scales_ref[...].T

    def centroids_tile(k):
        panel_copies[k // tile].wait()
        sq = jnp.zeros((tile, blk), jnp.float32)
        for b in range(n_blk):
            full = panel_ref[k:k + tile, b * blk:(b + 1) * blk].astype(jnp.float32)
            full = (full * scales[k:k + tile, b:b + 1]).astype(jnp.bfloat16)
            cent_ref[k:k + tile, b * blk:(b + 1) * blk] = full
            wide = full.astype(jnp.float32)
            sq = sq + wide * wide
        norm = jnp.sum(sq, axis=1, keepdims=True)
        bias_ref[k:k + tile, :] = jnp.broadcast_to((-0.5 * scale2) * norm, (tile, LANES))

    stat_copies = []

    def logits_tile(c, k):
        prod = lax.dot_general(cent_ref[k:k + tile, :], rows_ref[c * n:(c + 1) * n, :], NT,
                               preferred_element_type=jnp.float32)
        bias = jnp.concatenate([bias_ref[k:k + tile, :]] * (n // LANES), axis=1)
        t = prod * scale2 + bias
        t_refs[c][k:k + tile, :] = t
        return jnp.max(t.reshape(tile // 8, 8, n), axis=0)

    def exp_tile(c, k, top):
        e = jnp.exp2(t_refs[c][k:k + tile, :] - top)
        t_refs[c][k:k + tile, :] = e
        return jnp.sum(e.reshape(tile // 8, 8, n), axis=0)

    def send_stats(c, top, total):
        stat_out[c, 0:1, :] = top
        stat_out[c, 1:2, :] = total
        for o, peer in enumerate(z_peers):
            cp = pltpu.make_async_remote_copy(
                stat_out.at[c], stat_in.at[c, o], stat_ss.at[c, o], stat_rs.at[c, o],
                device_id={"cent": peer}, device_id_type=MESH)
            cp.start()
            stat_copies.append(cp)

    def ratios(c):
        for cp in stat_copies[c * len(z_peers):(c + 1) * len(z_peers)]:
            cp.wait_recv()
        mine = stat_out[c, 0:1, :]
        top = mine
        for o in range(len(z_peers)):
            top = jnp.maximum(top, stat_in[c, o, 0:1, :])
        total = stat_out[c, 1:2, :] * jnp.exp2(mine - top)
        for o in range(len(z_peers)):
            total = total + stat_in[c, o, 1:2, :] * jnp.exp2(stat_in[c, o, 0:1, :] - top)
        return jnp.exp2(mine - top) / total

    def weights_tile(c, k, ratio):
        w = t_refs[c][k:k + tile, :] * ratio
        w_ref[k:k + tile, c * n:(c + 1) * n] = w.astype(jnp.bfloat16)
        part = w[:, :LANES]
        for l in range(LANES, n, LANES):
            part = part + w[:, l:l + LANES]
        if c > 0:
            part = part + cnt_ref[k:k + tile, :]
        cnt_ref[k:k + tile, :] = part

    def weights(c, ratio):
        for k in range(0, n_cent, tile):
            weights_tile(c, k, ratio)

    tops = []
    centroids_tile(0)
    for c in range(n_chunks + 1):
        if c < n_chunks:
            row_copies[c].wait()
        if c >= 3:
            ratio = ratios(c - 3)
        best = total = None
        for k in range(0, n_cent, tile):
            if c == 0 and k + tile < n_cent:
                centroids_tile(k + tile)
            if c < n_chunks:
                m = logits_tile(c, k)
                best = m if best is None else jnp.maximum(best, m)
            if c > 0:
                part = exp_tile(c - 1, k, tops[c - 1])
                total = part if total is None else total + part
            if c >= 3:
                weights_tile(c - 3, k, ratio)
        if c < n_chunks:
            tops.append(jnp.max(best, axis=0, keepdims=True))
        if c == 1:
            pl.semaphore_wait(barrier, len(z_peers) + len(group))
        if c > 0:
            send_stats(c - 1, tops[c - 1], jnp.sum(total, axis=0, keepdims=True))

    def columns(q):
        return pl.ds(pl.multiple_of(flip(d, q, bits) * (2 * fb), 2 * fb), 2 * fb)

    core_copies = {}
    dp_copies = {}

    first = r == 0
    orders = [list(range(bits)), list(range(bits))[::-1]]

    def dot(start, stop, h, q):
        return lax.dot_general(w_ref[h * half:(h + 1) * half, start:stop],
                               rows_ref[start:stop, columns(q)], NN,
                               preferred_element_type=jnp.float32)

    def split(h, q, prod):
        own_ref[h, q] = jnp.where(first, prod[:, :fb], prod[:, fb:])
        core_out[h, q] = jnp.where(first, prod[:, fb:], prod[:, :fb]).astype(jnp.bfloat16)
        cp = pltpu.make_async_remote_copy(
            core_out.at[h, q], core_in.at[h, q], core_ss.at[h, q], core_rs.at[h, q],
            device_id={"rep": 1 - r}, device_id_type=MESH)
        cp.start()
        core_copies[h, q] = cp

    def finish(h, q):
        order = orders[h]
        j = first_step(q, order)
        core_copies[h, q].wait_recv()
        total = own_ref[h, q] + core_in[h, q].astype(jnp.float32)
        for i in range(j):
            src = q ^ (1 << order[i])
            dp_copies[h, src].wait_recv()
            total = total + dp_in[h, src - 1].astype(jnp.float32)
        if q == 0:
            out_ref[h * half:(h + 1) * half, :] = total
            return
        dp_out[h, q - 1] = total.astype(jnp.bfloat16)
        cp = pltpu.make_async_remote_copy(
            dp_out.at[h, q - 1], dp_in.at[h, q - 1], dp_ss.at[h, q - 1], dp_rs.at[h, q - 1],
            device_id={"dp": flip(d, 1 << order[j], bits)}, device_id_type=MESH)
        cp.start()
        dp_copies[h, q] = cp

    ranked = [sorted(range(dp_n), reverse=True, key=lambda q: [(q >> b) & 1 for b in order])
              for order in orders]

    q0 = ranked[0][0]
    known = n_chunks - 2
    steps = [(0, known * n)] + [(c * n, (c + 1) * n) for c in range(known, n_chunks)]
    for i, (start, stop) in enumerate(steps):
        if i > 0:
            c = known + i - 1
            weights(c, ratios(c))
        for h in range(2):
            prod = dot(start, stop, h, q0)
            if i > 0:
                prod = prod + early_ref[h]
            if i < len(steps) - 1:
                early_ref[h] = prod
            else:
                split(h, q0, prod)

    cnt_out[...] = jnp.sum(cnt_ref[...].T, axis=0, keepdims=True)
    cnt_copies = []
    for o, (pd, pr) in enumerate(group):
        cp = pltpu.make_async_remote_copy(
            cnt_out, cnt_in.at[o], cnt_ss.at[o], cnt_rs.at[o],
            device_id={"dp": pd, "rep": pr}, device_id_type=MESH)
        cp.start()
        cnt_copies.append(cp)

    for i in range(1, dp_n):
        for h in range(2):
            split(h, ranked[h][i], dot(0, n_rows, h, ranked[h][i]))
            finish(h, ranked[h][i - 1])

    counts = cnt_out[...]
    for o, cp in enumerate(cnt_copies):
        cp.wait_recv()
        counts = counts + cnt_in[o]
    counts_ref[...] = counts

    for h in range(2):
        finish(h, ranked[h][-1])

    for cp in stat_copies + cnt_copies + list(core_copies.values()) + list(dp_copies.values()):
        cp.wait_send()


def place(sums_ref, counts_in, out_ref, counts_ref):
    out_ref[...] = sums_ref[...].T
    counts_ref[...] = counts_in[...]


def on_device(sizes, rows, panel, scales, inv_temp):
    dp_n, cent_n, rep_n = sizes
    n_rows, width = rows.shape
    n_cent = panel.shape[0]
    n_chunks = 4
    tile = 256
    n = n_rows // n_chunks
    fb = width // (dp_n * rep_n)
    half = n_cent // 2
    group = dp_n * rep_n - 1
    f32, bf16 = jnp.float32, jnp.bfloat16
    dma = pltpu.SemaphoreType.DMA
    body = functools.partial(kernel, dp_n, cent_n, rep_n, (n_chunks, tile))
    sums, counts = pl.pallas_call(
        body,
        out_shape=(jax.ShapeDtypeStruct((n_cent, fb), f32), jax.ShapeDtypeStruct((1, n_cent), f32)),
        in_specs=[pl.BlockSpec(memory_space=pl.ANY), pl.BlockSpec(memory_space=pl.ANY),
                  pl.BlockSpec(memory_space=pltpu.VMEM), pl.BlockSpec(memory_space=pltpu.SMEM)],
        out_specs=(pl.BlockSpec(memory_space=pltpu.VMEM), pl.BlockSpec(memory_space=pltpu.VMEM)),
        scratch_shapes=[
            pltpu.VMEM((n_rows, width), bf16),
            pltpu.VMEM((n_cent, width), bf16),
            pltpu.VMEM((n_cent, width), bf16),
            pltpu.VMEM((n_cent, LANES), f32),
            pltpu.VMEM((n_cent, n_rows), bf16),
            pltpu.VMEM((n_cent, LANES), f32),
            *[pltpu.VMEM((n_cent, n), f32) for _ in range(n_chunks)],
            pltpu.VMEM((2, half, 2 * fb), f32),
            pltpu.VMEM((2, dp_n, half, fb), f32),
            pltpu.VMEM((2, dp_n, half, fb), bf16),
            pltpu.VMEM((2, dp_n, half, fb), bf16),
            pltpu.VMEM((2, dp_n - 1, half, fb), bf16),
            pltpu.VMEM((2, dp_n - 1, half, fb), bf16),
            pltpu.VMEM((n_chunks, 2, n), f32),
            pltpu.VMEM((n_chunks, cent_n - 1, 2, n), f32),
            pltpu.VMEM((1, n_cent), f32),
            pltpu.VMEM((group, 1, n_cent), f32),
            dma((n_chunks,)), dma((n_cent // tile,)),
            dma((2, dp_n)), dma((2, dp_n)),
            dma((2, dp_n - 1)), dma((2, dp_n - 1)),
            dma((n_chunks, cent_n - 1)), dma((n_chunks, cent_n - 1)),
            dma((group,)), dma((group,)),
        ],
        compiler_params=pltpu.CompilerParams(
            collective_id=0, has_side_effects=True, vmem_limit_bytes=56 * 1024 * 1024),
    )(rows, panel, scales.T, inv_temp)
    sums, counts = pl.pallas_call(
        place,
        out_shape=(jax.ShapeDtypeStruct((fb, n_cent), f32), jax.ShapeDtypeStruct((1, n_cent), f32)),
        in_specs=[pl.BlockSpec(memory_space=pltpu.VMEM)] * 2,
        out_specs=(pl.BlockSpec(memory_space=pltpu.VMEM),) * 2,
    )(sums, counts)
    return sums, counts.reshape(n_cent)


def solution(mesh):
    sizes = (mesh.shape["dp"], mesh.shape["cent"], mesh.shape["rep"])
    in_specs = (P(("dp", "rep"), None), P("cent", None), P("cent", None), P())
    out_specs = (P(("dp", "rep"), "cent"), P("cent"))
    return jax.shard_map(
        functools.partial(on_device, sizes), mesh=mesh, in_specs=in_specs, out_specs=out_specs,
        check_vma=False,
    )
```

```python
import functools
import math

import jax
import jax.numpy as jnp
from jax import lax
from jax.experimental import pallas as pl
from jax.experimental.pallas import tpu as pltpu
from jax.sharding import PartitionSpec as P

MESH = pl.DeviceIdType.MESH
NT = (((1,), (1,)), ((), ()))
NN = (((1,), (0,)), ((), ()))
LANES = 128


def flip(index, mask, bits):
    for b in range(bits):
        if (mask >> b) & 1:
            index = index + (1 << b) - (2 << b) * ((index // (1 << b)) % 2)
    return index


def first_step(q, order):
    for j, b in enumerate(order):
        if (q >> b) & 1:
            return j
    return len(order)


def kernel(dp_n, cent_n, rep_n, parts,
           rows_hbm, panel_hbm, scales_ref, temp_ref,
           out_ref, counts_ref, *scratch):
    n_chunks, tile = parts
    scratch = list(scratch)
    rows_ref, panel_ref, cent_ref, bias_ref, w_ref, cnt_ref = scratch[:6]
    t_refs = scratch[6:6 + n_chunks]
    (early_ref, own_ref, core_out, core_in, dp_out, dp_in, stat_out, stat_in, cnt_out, cnt_in,
     rows_sem, panel_sem, core_ss, core_rs, dp_ss, dp_rs, stat_ss, stat_rs,
     cnt_ss, cnt_rs) = scratch[6 + n_chunks:]

    n_rows, width = rows_ref.shape
    n_cent = cent_ref.shape[0]
    n = n_rows // n_chunks
    n_blk = scales_ref.shape[0]
    blk = width // n_blk
    fb = out_ref.shape[1]
    half = n_cent // 2
    bits = dp_n.bit_length() - 1

    d = lax.axis_index("dp")
    z = lax.axis_index("cent")
    r = lax.axis_index("rep")

    first_rows = pltpu.make_async_copy(
        rows_hbm.at[pl.ds(0, n)], rows_ref.at[pl.ds(0, n)], rows_sem.at[0])
    panel_copies = []
    for i, k in enumerate(range(0, n_cent, tile)):
        cp = pltpu.make_async_copy(
            panel_hbm.at[pl.ds(k, tile)], panel_ref.at[pl.ds(k, tile)], panel_sem.at[i])
        cp.start()
        panel_copies.append(cp)
        if i == 0:
            first_rows.start()
    row_copies = [first_rows]
    for c in range(1, n_chunks):
        cp = pltpu.make_async_copy(
            rows_hbm.at[pl.ds(c * n, n)], rows_ref.at[pl.ds(c * n, n)], rows_sem.at[c])
        cp.start()
        row_copies.append(cp)

    z_peers = [lax.rem(z + o, cent_n) for o in range(1, cent_n)]
    group = [(lax.rem(d + o // rep_n, dp_n), lax.rem(r + o % rep_n, rep_n))
             for o in range(1, dp_n * rep_n)]
    barrier = pltpu.get_barrier_semaphore()
    for peer in z_peers:
        pl.semaphore_signal(barrier, inc=1, device_id={"cent": peer}, device_id_type=MESH)
    for pd, pr in group:
        pl.semaphore_signal(barrier, inc=1, device_id={"dp": pd, "rep": pr}, device_id_type=MESH)

    scale2 = temp_ref[0].astype(jnp.float32) * (math.log2(math.e) / math.sqrt(width))

    scales = scales_ref[...].T

    def centroids_tile(k):
        panel_copies[k // tile].wait()
        sq = jnp.zeros((tile, blk), jnp.float32)
        for b in range(n_blk):
            full = panel_ref[k:k + tile, b * blk:(b + 1) * blk].astype(jnp.float32)
            full = (full * scales[k:k + tile, b:b + 1]).astype(jnp.bfloat16)
            cent_ref[k:k + tile, b * blk:(b + 1) * blk] = full
            wide = full.astype(jnp.float32)
            sq = sq + wide * wide
        norm = jnp.sum(sq, axis=1, keepdims=True)
        bias_ref[k:k + tile, :] = jnp.broadcast_to((-0.5 * scale2) * norm, (tile, LANES))

    stat_copies = []

    def logits_tile(c, k):
        prod = lax.dot_general(cent_ref[k:k + tile, :], rows_ref[c * n:(c + 1) * n, :], NT,
                               preferred_element_type=jnp.float32)
        bias = jnp.concatenate([bias_ref[k:k + tile, :]] * (n // LANES), axis=1)
        t = prod * scale2 + bias
        t_refs[c][k:k + tile, :] = t
        return jnp.max(t.reshape(tile // 8, 8, n), axis=0)

    def exp_tile(c, k, top):
        e = jnp.exp2(t_refs[c][k:k + tile, :] - top)
        t_refs[c][k:k + tile, :] = e
        return jnp.sum(e.reshape(tile // 8, 8, n), axis=0)

    def send_stats(c, top, total):
        stat_out[c, 0:1, :] = top
        stat_out[c, 1:2, :] = total
        for o, peer in enumerate(z_peers):
            cp = pltpu.make_async_remote_copy(
                stat_out.at[c], stat_in.at[c, o], stat_ss.at[c, o], stat_rs.at[c, o],
                device_id={"cent": peer}, device_id_type=MESH)
            cp.start()
            stat_copies.append(cp)

    def ratios(c):
        for cp in stat_copies[c * len(z_peers):(c + 1) * len(z_peers)]:
            cp.wait_recv()
        mine = stat_out[c, 0:1, :]
        top = mine
        for o in range(len(z_peers)):
            top = jnp.maximum(top, stat_in[c, o, 0:1, :])
        total = stat_out[c, 1:2, :] * jnp.exp2(mine - top)
        for o in range(len(z_peers)):
            total = total + stat_in[c, o, 1:2, :] * jnp.exp2(stat_in[c, o, 0:1, :] - top)
        return jnp.exp2(mine - top) / total

    def weights_tile(c, k, ratio):
        w = t_refs[c][k:k + tile, :] * ratio
        w_ref[k:k + tile, c * n:(c + 1) * n] = w.astype(jnp.bfloat16)
        part = w[:, :LANES]
        for l in range(LANES, n, LANES):
            part = part + w[:, l:l + LANES]
        if c > 0:
            part = part + cnt_ref[k:k + tile, :]
        cnt_ref[k:k + tile, :] = part

    def weights(c, ratio):
        for k in range(0, n_cent, tile):
            weights_tile(c, k, ratio)

    tops = []
    centroids_tile(0)
    for c in range(n_chunks + 1):
        if c < n_chunks:
            row_copies[c].wait()
        if c >= 3:
            ratio = ratios(c - 3)
        best = total = None
        for k in range(0, n_cent, tile):
            if c == 0 and k + tile < n_cent:
                centroids_tile(k + tile)
            if c < n_chunks:
                m = logits_tile(c, k)
                best = m if best is None else jnp.maximum(best, m)
            if c > 0:
                part = exp_tile(c - 1, k, tops[c - 1])
                total = part if total is None else total + part
            if c >= 3:
                weights_tile(c - 3, k, ratio)
        if c < n_chunks:
            tops.append(jnp.max(best, axis=0, keepdims=True))
        if c == 1:
            pl.semaphore_wait(barrier, len(z_peers) + len(group))
        if c > 0:
            send_stats(c - 1, tops[c - 1], jnp.sum(total, axis=0, keepdims=True))

    def columns(q):
        return pl.ds(pl.multiple_of(flip(d, q, bits) * (2 * fb), 2 * fb), 2 * fb)

    core_copies = {}
    dp_copies = {}

    first = r == 0
    orders = [list(range(bits)), list(range(bits))[::-1]]

    def dot(start, stop, h, q):
        return lax.dot_general(w_ref[h * half:(h + 1) * half, start:stop],
                               rows_ref[start:stop, columns(q)], NN,
                               preferred_element_type=jnp.float32)

    def split(h, q, prod):
        own_ref[h, q] = jnp.where(first, prod[:, :fb], prod[:, fb:])
        core_out[h, q] = jnp.where(first, prod[:, fb:], prod[:, :fb]).astype(jnp.bfloat16)
        cp = pltpu.make_async_remote_copy(
            core_out.at[h, q], core_in.at[h, q], core_ss.at[h, q], core_rs.at[h, q],
            device_id={"rep": 1 - r}, device_id_type=MESH)
        cp.start()
        core_copies[h, q] = cp

    def finish(h, q):
        order = orders[h]
        j = first_step(q, order)
        core_copies[h, q].wait_recv()
        total = own_ref[h, q] + core_in[h, q].astype(jnp.float32)
        for i in range(j):
            src = q ^ (1 << order[i])
            dp_copies[h, src].wait_recv()
            total = total + dp_in[h, src - 1].astype(jnp.float32)
        if q == 0:
            out_ref[h * half:(h + 1) * half, :] = total
            return
        dp_out[h, q - 1] = total.astype(jnp.bfloat16)
        cp = pltpu.make_async_remote_copy(
            dp_out.at[h, q - 1], dp_in.at[h, q - 1], dp_ss.at[h, q - 1], dp_rs.at[h, q - 1],
            device_id={"dp": flip(d, 1 << order[j], bits)}, device_id_type=MESH)
        cp.start()
        dp_copies[h, q] = cp

    ranked = [sorted(range(dp_n), reverse=True, key=lambda q: [(q >> b) & 1 for b in order])
              for order in orders]

    q0 = ranked[0][0]
    known = n_chunks - 2
    steps = [(0, known * n)] + [(c * n, (c + 1) * n) for c in range(known, n_chunks)]
    for i, (start, stop) in enumerate(steps):
        if i > 0:
            c = known + i - 1
            weights(c, ratios(c))
        for h in range(2):
            prod = dot(start, stop, h, q0)
            if i > 0:
                prod = prod + early_ref[h]
            if i < len(steps) - 1:
                early_ref[h] = prod
            else:
                split(h, q0, prod)

    cnt_out[...] = jnp.sum(cnt_ref[...].T, axis=0, keepdims=True)
    cnt_copies = []
    for o, (pd, pr) in enumerate(group):
        cp = pltpu.make_async_remote_copy(
            cnt_out, cnt_in.at[o], cnt_ss.at[o], cnt_rs.at[o],
            device_id={"dp": pd, "rep": pr}, device_id_type=MESH)
        cp.start()
        cnt_copies.append(cp)

    for i in range(1, dp_n):
        for h in range(2):
            finish(h, ranked[h][i - 1])
            split(h, ranked[h][i], dot(0, n_rows, h, ranked[h][i]))

    counts = cnt_out[...]
    for o, cp in enumerate(cnt_copies):
        cp.wait_recv()
        counts = counts + cnt_in[o]
    counts_ref[...] = counts

    for h in range(2):
        finish(h, ranked[h][-1])

    for cp in stat_copies + cnt_copies + list(core_copies.values()) + list(dp_copies.values()):
        cp.wait_send()


def place(sums_ref, counts_in, out_ref, counts_ref):
    out_ref[...] = sums_ref[...].T
    counts_ref[...] = counts_in[...]


def on_device(sizes, rows, panel, scales, inv_temp):
    dp_n, cent_n, rep_n = sizes
    n_rows, width = rows.shape
    n_cent = panel.shape[0]
    n_chunks = 4
    tile = 256
    n = n_rows // n_chunks
    fb = width // (dp_n * rep_n)
    half = n_cent // 2
    group = dp_n * rep_n - 1
    f32, bf16 = jnp.float32, jnp.bfloat16
    dma = pltpu.SemaphoreType.DMA
    body = functools.partial(kernel, dp_n, cent_n, rep_n, (n_chunks, tile))
    sums, counts = pl.pallas_call(
        body,
        out_shape=(jax.ShapeDtypeStruct((n_cent, fb), f32), jax.ShapeDtypeStruct((1, n_cent), f32)),
        in_specs=[pl.BlockSpec(memory_space=pl.ANY), pl.BlockSpec(memory_space=pl.ANY),
                  pl.BlockSpec(memory_space=pltpu.VMEM), pl.BlockSpec(memory_space=pltpu.SMEM)],
        out_specs=(pl.BlockSpec(memory_space=pltpu.VMEM), pl.BlockSpec(memory_space=pltpu.VMEM)),
        scratch_shapes=[
            pltpu.VMEM((n_rows, width), bf16),
            pltpu.VMEM((n_cent, width), bf16),
            pltpu.VMEM((n_cent, width), bf16),
            pltpu.VMEM((n_cent, LANES), f32),
            pltpu.VMEM((n_cent, n_rows), bf16),
            pltpu.VMEM((n_cent, LANES), f32),
            *[pltpu.VMEM((n_cent, n), f32) for _ in range(n_chunks)],
            pltpu.VMEM((2, half, 2 * fb), f32),
            pltpu.VMEM((2, dp_n, half, fb), f32),
            pltpu.VMEM((2, dp_n, half, fb), bf16),
            pltpu.VMEM((2, dp_n, half, fb), bf16),
            pltpu.VMEM((2, dp_n - 1, half, fb), bf16),
            pltpu.VMEM((2, dp_n - 1, half, fb), bf16),
            pltpu.VMEM((n_chunks, 2, n), f32),
            pltpu.VMEM((n_chunks, cent_n - 1, 2, n), f32),
            pltpu.VMEM((1, n_cent), f32),
            pltpu.VMEM((group, 1, n_cent), f32),
            dma((n_chunks,)), dma((n_cent // tile,)),
            dma((2, dp_n)), dma((2, dp_n)),
            dma((2, dp_n - 1)), dma((2, dp_n - 1)),
            dma((n_chunks, cent_n - 1)), dma((n_chunks, cent_n - 1)),
            dma((group,)), dma((group,)),
        ],
        compiler_params=pltpu.CompilerParams(
            collective_id=0, has_side_effects=True, vmem_limit_bytes=56 * 1024 * 1024),
    )(rows, panel, scales.T, inv_temp)
    sums, counts = pl.pallas_call(
        place,
        out_shape=(jax.ShapeDtypeStruct((fb, n_cent), f32), jax.ShapeDtypeStruct((1, n_cent), f32)),
        in_specs=[pl.BlockSpec(memory_space=pltpu.VMEM)] * 2,
        out_specs=(pl.BlockSpec(memory_space=pltpu.VMEM),) * 2,
    )(sums, counts)
    return sums, counts.reshape(n_cent)


def solution(mesh):
    sizes = (mesh.shape["dp"], mesh.shape["cent"], mesh.shape["rep"])
    in_specs = (P(("dp", "rep"), None), P("cent", None), P("cent", None), P())
    out_specs = (P(("dp", "rep"), "cent"), P("cent"))
    return jax.shard_map(
        functools.partial(on_device, sizes), mesh=mesh, in_specs=in_specs, out_specs=out_specs,
        check_vma=False,
    )
```
